32 devices in a mesh: seq: 16 (over z, x, core), tp: 2 (over y).
Axes of the slice: x: 2, y: 2, z: 4, core: 2. Of those that a mesh axis runs over, the one named last changes fastest.
Arguments:
- layer_input: bfloat16 [16384, 1024], P('seq'), may hold values from -6 to 6
- attn_gain: float32 [1024], replicated, may hold values from 0.5 to 1.5
- w_qkv: bfloat16 [1024, 3, 1024], P('seq', None, 'tp'), may hold values from -0.1875 to 0.1875
- w_out: bfloat16 [1024, 1024], P('tp', 'seq'), may hold values from -6 to 6
- mlp_gain: float32 [1024], replicated, may hold values from 0.5 to 1.5
- w_up: bfloat16 [1024, 4096], P('seq', 'tp'), may hold values from -0.1875 to 0.1875
- w_down: bfloat16 [4096, 1024], P('tp', 'seq'), may hold values from -0.09375 to 0.09375
- w_unpatch: bfloat16 [1024, 2048], P('seq'), may hold values from -0.1875 to 0.1875
- dens_in: float32 [64, 32], replicated, may hold values from -1 to 1
- dens_bias: float32 [64], replicated, may hold values from -3 to 3
- dens_out: float32 [64], replicated, may hold values from -0.75 to 0.75
- color_in: float32 [64, 32], replicated, may hold values from -1 to 1
- color_bias: float32 [64], replicated, may hold values from -3 to 3
- color_out: float32 [3, 64], replicated, may hold values from -0.75 to 0.75
- edge_ids: int32 [16, 2048], P('seq', 'tp'), may hold values from 0 to 393215
- blend_steps: int32 [16, 2048], P('seq', 'tp'), may hold values from 0 to 16
- live_count: int32 [16, 2], P('seq', 'tp'), may hold values from 256 to 1024, as said below
- color_grad: float32 [3, 16, 2048], P(None, 'seq', 'tp'), may hold values from -6 to 6
- out_grad: float32 [16384, 1024], P('seq'), may hold values from -6 to 6
Outputs:
- colors: float32 [3, 16, 2048], P(None, 'seq', 'tp')
- x_grad: float32 [16384, 1024], P(('seq', 'tp'))
- attn_gain_grad: float32 [1024], replicated
- w_qkv_grad: float32 [1024, 3, 1024], P('seq', None, 'tp')
- w_out_grad: float32 [1024, 1024], P('tp', 'seq')
- mlp_gain_grad: float32 [1024], replicated
- w_up_grad: float32 [1024, 4096], P('seq', 'tp')
- w_down_grad: float32 [4096, 1024], P('tp', 'seq')
- w_unpatch_grad: float32 [1024, 2048], P('seq')
- dens_in_grad: float32 [64, 32], replicated
- dens_bias_grad: float32 [64], replicated
- dens_out_grad: float32 [64], replicated
- color_in_grad: float32 [64, 32], replicated
- color_bias_grad: float32 [64], replicated
- color_out_grad: float32 [3, 64], replicated
The draws below stay inside these ranges and needn't reach their ends.
Inputs may be any that keep to these rules, and one draw needn't show every extreme that they name: `live_count`: in every scene some slab uses all 1024 slots of its list.
All inputs are finite; a program needn't handle non-finite values.
Results may differ from the reference program's by a relative error of at most 0.025.
The reference program's roundings to bfloat16 on the way count: a program that leaves them out, or rounds other values in their place, can miss the bound.
Values may be sent and summed in bfloat16 or wider, within the bound.
No kernel may reach another device: no remote copies, remote signals or barrier semaphores. Data moves between devices by JAX's collectives and lax.ppermute only.
A program may use at most 512 MiB of HBM per device.

```python
import jax
import jax.numpy as jnp
from jax import lax

D = 1024
HEADS = 16
HEAD_DIM = 64
FF = 4096
FEAT = 32
DENS = 64
COLOR = 64
PATCH = 8
SCENE = 1024
GRID = 64
PIX = 1024
TOKENS = 16384
TRI = 192
SLAB = 32
N_SEQ = 16
N_TP = 2


def draw_live_count(key, part):
    count_key, full_key = jax.random.split(key)
    counts = jax.random.randint(count_key, (N_SEQ, N_TP), PIX // 4, PIX + 1)
    full_slab = jax.random.randint(full_key, (N_SEQ, 1), 0, N_TP)
    slab_ids = jnp.arange(N_TP, dtype=jnp.int32)[None, :]
    return jnp.where(slab_ids == full_slab, PIX, counts).astype(jnp.int32)


def set_ends(drawn, key, low, largest):
    shape = drawn.shape
    index_at = [jax.random.randint(jax.random.fold_in(key, axis), (), 0, shape[axis]) for axis in range(len(shape))]
    drawn = drawn.at[tuple(index_at)].set(low)
    longest = shape.index(max(shape))
    index_at[longest] = (index_at[longest] + 1) % shape[longest]
    return drawn.at[tuple(index_at)].set(largest)


def block_levels(stream_key, shape, cuts, smallest, top_value):
    gain = 1.0
    for axis_at, blocks in cuts:
        draws = jax.random.uniform(jax.random.fold_in(jax.random.fold_in(stream_key, 6), axis_at), (blocks,), jnp.float32, smallest / len(cuts), top_value / len(cuts))
        gain = gain * jnp.repeat(jnp.exp(draws), shape[axis_at] // blocks).reshape((-1,) + (1,) * (len(shape) - 1 - axis_at))
    return gain


def bell_draw(rng, dims, width, most, cuts=(), kind=jnp.bfloat16):
    result = jax.random.normal(rng, dims, jnp.float32) * width
    if len(cuts) > 0:
        result = block_levels(rng, dims, cuts, -0.22, 0.18) * result
    return jnp.clip(result, min=-most, max=most).astype(kind)


def setup_inputs(seed: int = 0) -> dict:
    arg_keys = jax.random.split(jax.random.key(seed), 20)
    return {
        "layer_input": bell_draw(arg_keys[0], (TOKENS, D), 1.0, 6.0, ((0, 16),)),
        "attn_gain": jnp.clip(1.0 + 0.1 * jax.random.normal(arg_keys[1], (D,), jnp.float32), 0.5, 1.5),
        "w_qkv": bell_draw(arg_keys[2], (D, 3, D), D ** -0.5, 0.1875, ((0, 16), (2, 2))),
        "w_out": bell_draw(arg_keys[3], (D, D), 1.0, 6.0, ((0, 2), (1, 16))),
        "mlp_gain": jnp.clip(1.0 + 0.1 * jax.random.normal(arg_keys[4], (D,), jnp.float32), 0.5, 1.5),
        "w_up": bell_draw(arg_keys[5], (D, FF), D ** -0.5, 0.1875, ((0, 16), (1, 2))),
        "w_down": bell_draw(arg_keys[6], (FF, D), FF ** -0.5, 0.09375, ((0, 2), (1, 16))),
        "w_unpatch": bell_draw(arg_keys[7], (D, PATCH * PATCH * FEAT), D ** -0.5, 0.1875, ((0, 16),)),
        "dens_in": bell_draw(arg_keys[8], (DENS, FEAT), FEAT ** -0.5, 1.0, (), jnp.float32),
        "dens_bias": bell_draw(arg_keys[9], (DENS,), 0.5, 3.0, (), jnp.float32),
        "dens_out": bell_draw(arg_keys[10], (DENS,), DENS ** -0.5, 0.75, (), jnp.float32),
        "color_in": bell_draw(arg_keys[11], (COLOR, FEAT), FEAT ** -0.5, 1.0, (), jnp.float32),
        "color_bias": bell_draw(arg_keys[12], (COLOR,), 0.5, 3.0, (), jnp.float32),
        "color_out": bell_draw(arg_keys[13], (3, COLOR), COLOR ** -0.5, 0.75, (), jnp.float32),
        "edge_ids": set_ends(jax.random.randint(arg_keys[14], (N_SEQ, N_TP * PIX), 0, 3 * SLAB * GRID * GRID), jax.random.fold_in(arg_keys[14], 1), 0, (3 * SLAB * GRID * GRID) - 1).astype(jnp.int32),
        "blend_steps": set_ends(jax.random.randint(arg_keys[15], (N_SEQ, N_TP * PIX), 0, 17), jax.random.fold_in(arg_keys[15], 1), 0, 16).astype(jnp.int32),
        "live_count": draw_live_count(jax.random.fold_in(arg_keys[19], 71), 0),
        "color_grad": bell_draw(arg_keys[17], (3, N_SEQ, N_TP * PIX), 1.0, 6.0, ((1, 16), (2, 2)), jnp.float32),
        "out_grad": bell_draw(arg_keys[18], (TOKENS, D), 1.0, 6.0, ((0, 16),), jnp.float32),
    }


HIGHEST = lax.Precision.HIGHEST

@jax.custom_vjp
def low(v):
    return lax.optimization_barrier(v.astype(jnp.bfloat16)).astype(jnp.float32)

@jax.custom_vjp
def low_back(v):
    return v

def low_keep(v):
    return (low(v), None)

def low_pass(kept, grad):
    return (grad,)

def back_keep(v):
    return (v, None)

def back_low(kept, grad):
    return (low(grad),)
low.defvjp(low_keep, low_pass)
low_back.defvjp(back_keep, back_low)

def both_ways(values):
    return low(low_back(values))

def gelu_exact(values):
    return jax.nn.gelu(values, approximate=False)

def layer_norm(values, gain_vec):
    center = values - lax.optimization_barrier(jnp.mean(values, axis=-1, keepdims=True))
    spread = lax.optimization_barrier(jnp.mean(center * center, axis=-1, keepdims=True))
    return center * lax.rsqrt(spread + 1e-05) * gain_vec

def density(field_vals, dens_in, dens_bias, dens_out):
    hidden = gelu_exact(jnp.dot(dens_in, field_vals, precision=HIGHEST) + dens_bias[:, None])
    return jnp.dot(dens_out, hidden, precision=HIGHEST)

def decode(vertex_feat, vertex_dens, color_in, color_bias, color_out):
    hidden = gelu_exact(jnp.dot(color_in, vertex_feat, precision=HIGHEST) + color_bias[:, None])
    shade_rgb = jax.nn.sigmoid(jnp.dot(color_out, hidden, precision=HIGHEST))
    return jax.nn.sigmoid(vertex_dens)[None, :] * shade_rgb

def edge_ends(edge_row, slab_planes, grid_side, plane_offset):
    slab_cells = slab_planes * grid_side * grid_side
    direction = edge_row // slab_cells
    cell_index = edge_row % slab_cells
    plane_a = cell_index // (grid_side * grid_side) + plane_offset
    spot_a = cell_index % (grid_side * grid_side)
    column = spot_a // grid_side
    depth_index = spot_a % grid_side
    valid_mask = (direction == 0) | (direction == 1) & (column < grid_side - 1) | (direction == 2) & (depth_index < grid_side - 1)
    plane_b = jnp.where(direction == 0, plane_a + 1, plane_a)
    spot_b = jnp.where(valid_mask & (direction == 1), spot_a + grid_side, jnp.where(valid_mask & (direction == 2), spot_a + 1, spot_a))
    return (plane_a, spot_a, plane_b, spot_b, valid_mask.astype(jnp.float32))

def attention(queries, key_rows, value_rows):
    block_rows = min(512, SCENE)
    score_scale = HEAD_DIM ** (-0.5)

    def one_block(q_block):
        scores = low_back(jnp.einsum('qhd,khd->hqk', q_block, key_rows, precision=HIGHEST) * score_scale)
        probs = low(jax.nn.softmax(scores, axis=-1))
        return jnp.einsum('hqk,khd->qhd', probs, value_rows, precision=HIGHEST)
    blocks_out = lax.map(jax.checkpoint(one_block), queries.reshape(SCENE // block_rows, block_rows, HEADS, HEAD_DIM))
    return blocks_out.reshape(SCENE, HEADS * HEAD_DIM)

def scene_colors(params_all, scene_in):
    attn_gain, w_qkv, w_out, mlp_gain, w_up, w_down, w_unpatch, dens_in, dens_bias, dens_out, color_in, color_bias, color_out = params_all
    scene_rows, edge_row, blend_row, count_row = scene_in
    normed_a = low(layer_norm(scene_rows, attn_gain))
    projected = jnp.einsum('td,dpe->tpe', normed_a, w_qkv, precision=HIGHEST)
    queries = both_ways(projected[:, 0]).reshape(SCENE, HEADS, HEAD_DIM)
    key_rows = both_ways(projected[:, 1]).reshape(SCENE, HEADS, HEAD_DIM)
    value_rows = both_ways(projected[:, 2]).reshape(SCENE, HEADS, HEAD_DIM)
    attended = both_ways(attention(queries, key_rows, value_rows))
    hidden = scene_rows + low_back(jnp.dot(attended, w_out, precision=HIGHEST))
    normed_b = low(layer_norm(hidden, mlp_gain))
    up_value = low_back(jnp.dot(normed_b, w_up, precision=HIGHEST))
    activated = low(gelu_exact(up_value))
    output = hidden + low_back(jnp.dot(activated, w_down, precision=HIGHEST))
    block_rows = SCENE // N_TP
    tri_rows = TRI // N_TP
    tokens_tri = low(output.reshape(N_TP, block_rows, D)[:, block_rows - tri_rows:].reshape(TRI, D))
    units = low_back(jnp.dot(tokens_tri, w_unpatch, precision=HIGHEST))
    grid_patches = GRID // PATCH
    planes = units.reshape(3, grid_patches, grid_patches, PATCH, PATCH, FEAT).transpose(0, 5, 1, 3, 2, 4).reshape(3, FEAT, GRID, GRID)

    def plane_forward(row_pair):
        field_vals = (row_pair[0][:, :, None] + row_pair[1][:, None, :] + planes[2]).reshape(FEAT, GRID * GRID)
        return (field_vals, density(field_vals, dens_in, dens_bias, dens_out))
    fields, densities = lax.map(jax.checkpoint(plane_forward), (jnp.transpose(planes[0], (1, 0, 2)), jnp.transpose(planes[1], (1, 0, 2))))
    field_ext = jnp.concatenate([fields, jnp.zeros((1, FEAT, GRID * GRID), jnp.float32)], 0)
    dens_ext = jnp.concatenate([densities, jnp.zeros((1, GRID * GRID), jnp.float32)], 0)
    entry = jnp.arange(N_TP * PIX, dtype=jnp.int32)
    slab_of = entry // PIX
    plane_a, spot_a, plane_b, spot_b, valid_b = edge_ends(edge_row, SLAB, GRID, slab_of * SLAB)
    weight_b = blend_row.astype(jnp.float32) / 16.0
    weight_a = 1.0 - weight_b
    weight_b = weight_b * valid_b
    live_mask = (entry % PIX < count_row[slab_of]).astype(jnp.float32)
    vertex_feat = (weight_a[:, None] * field_ext[plane_a, :, spot_a] + weight_b[:, None] * field_ext[plane_b, :, spot_b]).T
    vertex_dens = weight_a * dens_ext[plane_a, spot_a] + weight_b * dens_ext[plane_b, spot_b]
    return (live_mask[None, :] * decode(vertex_feat, vertex_dens, color_in, color_bias, color_out), output)

def reference(layer_input, attn_gain, w_qkv, w_out, mlp_gain, w_up, w_down, w_unpatch, dens_in, dens_bias, dens_out, color_in, color_bias, color_out, edge_ids, blend_steps, live_count, color_grad, out_grad):
    input_f32 = layer_input.astype(jnp.float32)
    params_all = (attn_gain, w_qkv.astype(jnp.float32), w_out.astype(jnp.float32), mlp_gain, w_up.astype(jnp.float32), w_down.astype(jnp.float32), w_unpatch.astype(jnp.float32), dens_in, dens_bias, dens_out, color_in, color_bias, color_out)

    def forward(input_vals, params_now):

        def one_scene(scene_in):
            return scene_colors(params_now, scene_in)
        per_scene, outputs = lax.map(jax.checkpoint(one_scene), (input_vals.reshape(N_SEQ, SCENE, D), edge_ids, blend_steps, live_count))
        return (jnp.transpose(per_scene, (1, 0, 2)), outputs.reshape(N_SEQ * SCENE, D))
    results, back_fn = jax.vjp(forward, input_f32, params_all)
    grad_input, grads = back_fn((color_grad, out_grad))
    return (results[0], grad_input, grads[0], grads[1], grads[2], grads[3], grads[4], grads[5], grads[6], grads[7], grads[8], grads[9], grads[10], grads[11], grads[12])
```

```python
import functools
import math

import jax
import jax.numpy as jnp
from jax import lax
from jax.experimental import pallas as pl
from jax.experimental.pallas import tpu as pltpu
from jax.sharding import PartitionSpec as P

HEAD_DIM = 64
FEAT = 32
PATCH = 8
GRID = 64
TRI = 192
SIDE = GRID // PATCH
PLANE_TOKENS = SIDE * SIDE
SPOTS = PLANE_TOKENS * PATCH
CELLS = PATCH * FEAT

HIGHEST = lax.Precision.HIGHEST
BF16 = jnp.bfloat16
F32 = jnp.float32
NN = (((1,), (0,)), ((), ()))
NT = (((1,), (1,)), ((), ()))
TN = (((0,), (0,)), ((), ()))


def cost(flops, moved, exps=0):
    return pl.CostEstimate(flops=int(flops), bytes_accessed=int(moved), transcendentals=int(exps))


def dot(a, b, dims=NN, precision=None):
    return lax.dot_general(a, b, dims, precision=precision, preferred_element_type=F32)


def gelu_parts(x):
    density = jnp.exp(-0.5 * x * x)
    t = 1.0 / (1.0 + (0.3275911 * 2.0**-0.5) * jnp.abs(x))
    poly = ((((1.061405429 * t - 1.453152027) * t + 1.421413741) * t - 0.284496736) * t + 0.254829592) * t
    tail = 0.5 * poly * density
    cdf = jnp.where(x < 0.0, tail, 1.0 - tail)
    return x * cdf, cdf + x * (density * (1.0 / math.sqrt(2.0 * math.pi)))


def leave(*refs):
    pass


def after(x, *others):
    if not others:
        return x
    anywhere = pl.BlockSpec(memory_space=pl.ANY)
    return pl.pallas_call(
        leave,
        in_specs=[anywhere] * (1 + len(others)),
        out_specs=anywhere,
        out_shape=jax.ShapeDtypeStruct(x.shape, x.dtype),
        input_output_aliases={0: 0},
        name="after",
    )(x, *others)


def layer_norm(values, gain_vec):
    center = values - jnp.mean(values, axis=-1, keepdims=True)
    spread = jnp.mean(center * center, axis=-1, keepdims=True)
    return center * lax.rsqrt(spread + 1e-05) * gain_vec


def attend_fwd_kernel(q_ref, k_ref, v_ref, o_ref, lse_ref, *, scale, block):
    length, width = q_ref.shape
    heads = width // HEAD_DIM
    lane = lax.broadcasted_iota(jnp.int32, (1, width), 1) // HEAD_DIM
    lane_block = lax.broadcasted_iota(jnp.int32, (block, width), 1)
    keys = k_ref[...]
    values = v_ref[...]
    zero = jnp.zeros((), BF16)
    masked = [jnp.where(lane == h, keys, zero) for h in range(heads)]
    for b in range(length // block):
        rows = pl.ds(b * block, block)
        q = (q_ref[rows, :].astype(F32) * scale).astype(BF16)
        result = jnp.zeros((block, width), F32)
        stats = jnp.zeros((block, width), F32)
        for h in range(heads):
            s = dot(q, masked[h], NT)
            top = jnp.max(s, axis=1, keepdims=True)
            p = jnp.exp(s - top)
            total = jnp.sum(p, axis=1, keepdims=True)
            o = dot((p * (1.0 / total)).astype(BF16), values)
            result = jnp.where(lane == h, o, result)
            stats = jnp.where(lane_block == h, top + jnp.log(total), stats)
        o_ref[rows, :] = result.astype(BF16)
        lse_ref[0, :, pl.ds(b * block, block)] = stats.T[:8, :]


def attend_fwd(projected, local_width):
    length = projected.shape[0]
    width = 2 * HEAD_DIM
    pairs = local_width // width
    spec = lambda part: pl.BlockSpec((length, width), lambda i: (0, part * pairs + i))
    return pl.pallas_call(
        functools.partial(attend_fwd_kernel, scale=HEAD_DIM**-0.5, block=512),
        grid=(pairs,),
        in_specs=[spec(0), spec(1), spec(2)],
        out_specs=[
            pl.BlockSpec((length, width), lambda i: (0, i)),
            pl.BlockSpec((1, 8, length), lambda i: (i, 0, 0)),
        ],
        out_shape=[
            jax.ShapeDtypeStruct((length, local_width), BF16),
            jax.ShapeDtypeStruct((pairs, 8, length), F32),
        ],
        compiler_params=pltpu.CompilerParams(vmem_limit_bytes=48 * 1024 * 1024),
        cost_estimate=cost(
            12 * length * length * local_width, 8 * length * local_width, length * length * pairs * 2
        ),
        name="attend_fwd",
    )(projected, projected, projected)


def attend_bwd_kernel(
    q_ref, k_ref, v_ref, g_ref, o_ref, lse_ref, out_ref, dq_ref, dk_ref, dv_ref, *, scale, block
):
    length, width = q_ref.shape
    heads = width // HEAD_DIM
    step = pl.program_id(1)

    @pl.when(step == 0)
    def _():
        lane = lax.broadcasted_iota(jnp.int32, (1, width), 1) // HEAD_DIM
        keys = k_ref[...]
        values = v_ref[...]
        zero = jnp.zeros((), BF16)
        key_cols = keys.T
        prod = g_ref[...].astype(F32) * o_ref[...].astype(F32)
        pick = (
            lax.broadcasted_iota(jnp.int32, (8, width), 1) // HEAD_DIM
            == lax.broadcasted_iota(jnp.int32, (8, width), 0)
        ).astype(F32)
        inner = dot(pick, prod, NT, HIGHEST)
        for h in range(heads):
            k_h = jnp.where(lane == h, keys, zero)
            v_h = jnp.where(lane == h, values, zero)
            for b in range(length // block):
                rows = pl.ds(b * block, block)
                q = (q_ref[rows, :].astype(F32) * scale).astype(BF16)
                g = g_ref[rows, :]
                s = dot(k_h, q, NT)
                p = jnp.exp(s - lse_ref[0, h : h + 1, b * block : (b + 1) * block])
                dp = dot(v_h, g, NT)
                ds = (p * (dp - inner[h : h + 1, b * block : (b + 1) * block])).astype(BF16)
                dv = dot(p.astype(BF16), jnp.where(lane == h, g, zero))
                dk = dot(ds, jnp.where(lane == h, q, zero))
                if h == 0 and b == 0:
                    dv_ref[...] = dv
                    dk_ref[...] = dk
                else:
                    dv_ref[...] += dv
                    dk_ref[...] += dk
                dq_ref[h * HEAD_DIM : (h + 1) * HEAD_DIM, b * block : (b + 1) * block] = (
                    dot(key_cols[h * HEAD_DIM : (h + 1) * HEAD_DIM, :], ds) * scale
                )
        out_ref[...] = dq_ref[...].T.astype(BF16)

    @pl.when(step == 1)
    def _():
        out_ref[...] = dk_ref[...].astype(BF16)

    @pl.when(step == 2)
    def _():
        out_ref[...] = dv_ref[...].astype(BF16)


def attend_bwd(projected, grad_heads, attended, lse, local_width):
    length = projected.shape[0]
    width = 2 * HEAD_DIM
    pairs = local_width // width
    spec = lambda part: pl.BlockSpec((length, width), lambda i, j: (0, part * pairs + i))
    return pl.pallas_call(
        functools.partial(attend_bwd_kernel, scale=HEAD_DIM**-0.5, block=256),
        grid=(pairs, 3),
        in_specs=[
            spec(0),
            spec(1),
            spec(2),
            spec(0),
            spec(0),
            pl.BlockSpec((1, 8, length), lambda i, j: (i, 0, 0)),
        ],
        out_specs=pl.BlockSpec((length, width), lambda i, j: (0, j * pairs + i)),
        out_shape=jax.ShapeDtypeStruct((length, 3 * local_width), BF16),
        scratch_shapes=[
            pltpu.VMEM((width, length), F32),
            pltpu.VMEM((length, width), F32),
            pltpu.VMEM((length, width), F32),
        ],
        compiler_params=pltpu.CompilerParams(vmem_limit_bytes=48 * 1024 * 1024),
        cost_estimate=cost(
            24 * length * length * local_width, 16 * length * local_width, length * length * pairs * 2
        ),
        name="attend_bwd",
    )(projected, projected, projected, grad_heads, attended, lse)


def mlp_mid_kernel(nb_ref, gm_ref, up_ref, down_ref, act_ref, gup_ref, *, block):
    up = up_ref[...]
    down = down_ref[...]
    for b in range(nb_ref.shape[0] // block):
        rows = pl.ds(b * block, block)
        value, slope = gelu_parts(dot(nb_ref[rows, :], up))
        act_ref[rows, :] = value.astype(BF16)
        gup_ref[rows, :] = (slope * dot(gm_ref[rows, :], down)).astype(BF16)


def mlp_mid(normed, grad, up_full, down_full):
    rows, depth = normed.shape
    width = up_full.shape[1]
    cols = min(width, 512)
    block = rows
    for cand in (416, 192):
        if rows % cand == 0:
            block = cand
            break
    whole = pl.BlockSpec((rows, depth), lambda i: (0, 0))
    weight = pl.BlockSpec((depth, cols), lambda i: (0, i))
    result = pl.BlockSpec((rows, cols), lambda i: (0, i))
    return pl.pallas_call(
        functools.partial(mlp_mid_kernel, block=block),
        grid=(width // cols,),
        in_specs=[whole, whole, weight, weight],
        out_specs=[result, result],
        out_shape=[jax.ShapeDtypeStruct((rows, width), BF16)] * 2,
        compiler_params=pltpu.CompilerParams(vmem_limit_bytes=48 * 1024 * 1024),
        cost_estimate=cost(
            8 * rows * depth * width, 4 * (rows + width) * depth + 4 * rows * width, rows * width
        ),
        name="mlp_mid",
    )(normed, grad, up_full, down_full)


def mlp_tri_kernel(nb_ref, up_ref, down_ref, out_ref):
    value, _ = gelu_parts(dot(nb_ref[...], up_ref[...]))
    part = dot(value.astype(BF16), down_ref[...], NT)

    @pl.when(pl.program_id(0) == 0)
    def _():
        out_ref[...] = part

    @pl.when(pl.program_id(0) > 0)
    def _():
        out_ref[...] += part


def mlp_tri(normed, up_full, down_full):
    rows, depth = normed.shape
    width = up_full.shape[1]
    cols = min(width, 512)
    whole = pl.BlockSpec((rows, depth), lambda i: (0, 0))
    weight = pl.BlockSpec((depth, cols), lambda i: (0, i))
    return pl.pallas_call(
        mlp_tri_kernel,
        grid=(width // cols,),
        in_specs=[whole, weight, weight],
        out_specs=whole,
        out_shape=jax.ShapeDtypeStruct((rows, depth), F32),
        compiler_params=pltpu.CompilerParams(vmem_limit_bytes=32 * 1024 * 1024),
        cost_estimate=cost(4e9, 4 * width * depth, rows * width),
        name="mlp_tri",
    )(normed, up_full, down_full)


def weight_grad_kernel(place_ref, *refs, segments, pieces):
    step = pl.program_id(0)
    rest = refs[2 * sum(n for n, _, _ in segments) :]
    outs, turned = rest[:pieces], rest[pieces:]
    at = 0
    for parts, first, last in segments:
        lefts, rights = refs[at : at + parts], refs[at + parts : at + 2 * parts]
        at += 2 * parts

        @pl.when(step == first)
        def _():
            for left, spot in zip(lefts, turned):
                rows = left.shape[0]
                for j in range(left.shape[1] // 128):
                    both = left[:, j * 128 : (j + 1) * 128].T
                    for k in range(2):
                        to = pl.multiple_of(place_ref[2 * j + k] * 64, 64)
                        spot[pl.ds(to, 64), :rows] = both[k * 64 : (k + 1) * 64]

        @pl.when((step >= first) & (step <= last))
        def _():
            total = sum(
                dot(spot[:, : right.shape[0]], right[...]) for spot, right in zip(turned, rights)
            )
            for i, out in enumerate(outs):
                rows = out.shape[0]
                out[...] = total[i * rows : (i + 1) * rows].astype(BF16)


def weight_grad(place, pieces, *segments):
    specs, args, marks = [], [], []
    first = 0
    cols = min(512, *(rights[0].shape[1] for _, rights in segments))
    depth = segments[0][0][0].shape[1]
    for lefts, rights in segments:
        steps = rights[0].shape[1] // cols
        for left in lefts:
            specs.append(pl.BlockSpec(left.shape, lambda i, place: (0, 0)))
            args.append(left)
        for right in rights:
            specs.append(
                pl.BlockSpec(
                    (right.shape[0], cols),
                    lambda i, place, a=first, b=steps: (0, jnp.clip(i - a, 0, b - 1)),
                )
            )
            args.append(right)
        marks.append((len(lefts), first, first + steps - 1))
        first += steps
    parts = segments[0][0]
    result = jax.ShapeDtypeStruct((depth // pieces, first * cols), BF16)
    return pl.pallas_call(
        functools.partial(weight_grad_kernel, segments=tuple(marks), pieces=pieces),
        grid_spec=pltpu.PrefetchScalarGridSpec(
            num_scalar_prefetch=1,
            grid=(first,),
            in_specs=specs,
            out_specs=[pl.BlockSpec((depth // pieces, cols), lambda i, place: (0, i))] * pieces,
            scratch_shapes=[pltpu.VMEM((depth, left.shape[0]), BF16) for left in parts],
        ),
        out_shape=[result] * pieces,
        compiler_params=pltpu.CompilerParams(vmem_limit_bytes=40 * 1024 * 1024),
        cost_estimate=cost(
            3 * depth * first * cols * sum(left.shape[0] for left in parts), 8 * depth * first * cols
        ),
        name="weight_grad",
    )(place, *args)


def split_halves(x):
    high = x.astype(BF16)
    return high, (x - high.astype(F32)).astype(BF16)


def dot_fine(a, b):
    a_high, a_low = split_halves(a)
    b_high, b_low = split_halves(b)
    return dot(
        jnp.concatenate([a_high, a_high, a_low], axis=1),
        jnp.concatenate([b_high, b_low, b_high], axis=0),
    )


def dot_fine_lanes(a, b):
    rows, cols = a.shape[0], b.shape[0]
    both = dot(
        jnp.concatenate(split_halves(a), axis=0), jnp.concatenate(split_halves(b), axis=0), NT
    )
    return both[:rows, :cols] + both[:rows, cols:] + both[rows:, :cols]


def scene_kernel(
    own_ref,
    tokens_ref,
    w_ref,
    spot_ref,
    edge_ref,
    cot_ref,
    net_ref,
    colors_ref,
    units_ref,
    gtok_ref,
    gdi_ref,
    gdb_ref,
    gdo_ref,
    gci_ref,
    gcb_ref,
    gco_ref,
    table_ref,
    hot_ref,
    grad_ref,
    *,
    per_slab,
):
    step = pl.program_id(0)
    block = spot_ref.shape[1]
    ends = 2 * block

    @pl.when(step == 0)
    def _():
        units = dot(tokens_ref[...], w_ref[...])
        for p in range(3):
            rows = jnp.concatenate(
                [
                    units[p * PLANE_TOKENS : (p + 1) * PLANE_TOKENS, r * CELLS : (r + 1) * CELLS]
                    for r in range(PATCH)
                ],
                axis=0,
            )
            high, low = split_halves(rows.T)
            table_ref[p, :CELLS, :] = high
            table_ref[p, CELLS:, :] = low
        grad_ref[...] = jnp.zeros_like(grad_ref)
        for ref in (gdi_ref, gdb_ref, gdo_ref, gci_ref, gcb_ref, gco_ref):
            ref[...] = jnp.zeros_like(ref)

    net = net_ref[...]
    dens_in, color_in = net[:, :FEAT], net[:, FEAT : 2 * FEAT]
    color_out_t = net[:, 2 * FEAT : 2 * FEAT + 8]
    at = 2 * FEAT + 8
    dens_bias, dens_out, color_bias = net[:, at : at + 1], net[:, at + 1 : at + 2], net[:, at + 2 : at + 3]
    dens_in_t, color_in_t, color_out = dens_in.T, color_in.T, color_out_t.T
    iota = lax.broadcasted_iota(jnp.int32, (SPOTS, ends), 0)
    field = jnp.zeros((FEAT, ends), F32)
    columns = []
    for p in range(3):
        spot = jnp.concatenate([spot_ref[p : p + 1, :], spot_ref[3 + p : 4 + p, :]], axis=1)
        column = jnp.concatenate([spot_ref[6 + p : 7 + p, :], spot_ref[9 + p : 10 + p, :]], axis=1)
        columns.append(column)
        hot = jnp.where(iota == spot, 1.0, 0.0).astype(BF16)
        hot_ref[p] = hot
        found = dot(table_ref[p], hot)
        found = found[:CELLS] + found[CELLS:]
        for c in range(PATCH):
            field = field + jnp.where(column == c, found[c * FEAT : (c + 1) * FEAT], 0.0)

    w_a = edge_ref[0:1, :]
    w_b = edge_ref[1:2, :]
    inside = edge_ref[2:3, :]
    live = edge_ref[3:4, :]
    pre_d = dot_fine(dens_in, field) + dens_bias
    act_d, slope_d = gelu_parts(pre_d)
    dens = jnp.sum(act_d * dens_out, axis=0, keepdims=True)
    v_dens = w_a * dens[:, :block] + w_b * inside * dens[:, block:]
    v_feat = w_a * field[:, :block] + w_b * field[:, block:]
    pre_c = dot_fine(color_in, v_feat) + color_bias
    act_c, slope_c = gelu_parts(pre_c)
    shade = jax.nn.sigmoid(dot_fine(color_out, act_c))
    opacity = jax.nn.sigmoid(v_dens)
    colors_ref[...] = live * opacity * shade
    g_color = cot_ref[...] * live
    g_shade = g_color * opacity
    g_logit = g_shade * shade * (1.0 - shade)
    g_dens = jnp.sum(g_color * shade, axis=0, keepdims=True) * opacity * (1.0 - opacity)
    g_pre_c = dot_fine(color_out_t, g_logit) * slope_c
    g_feat = dot_fine(color_in_t, g_pre_c)
    g_dens2 = jnp.concatenate([w_a * g_dens, w_b * inside * g_dens], axis=1)
    g_pre_d = dens_out * g_dens2 * slope_d
    g_field = dot_fine(dens_in_t, g_pre_d) + jnp.concatenate(
        [w_a * g_feat, w_b * g_feat], axis=1
    )

    @pl.when(step // per_slab == own_ref[0])
    def _():
        gco_ref[...] += dot_fine_lanes(g_logit, act_c)
        gci_ref[...] += dot_fine_lanes(g_pre_c, v_feat)
        gcb_ref[...] += jnp.sum(g_pre_c, axis=1, keepdims=True)
        gdi_ref[...] += dot_fine_lanes(g_pre_d, field)
        gdb_ref[...] += jnp.sum(g_pre_d, axis=1, keepdims=True)
        gdo_ref[...] += jnp.sum(act_d * g_dens2, axis=1, keepdims=True)

    for p in range(3):
        spread = jnp.concatenate(
            [jnp.where(columns[p] == c, g_field, 0.0) for c in range(PATCH)], axis=0
        )
        grad_ref[p] += dot(hot_ref[p], spread.astype(BF16), NT)

    @pl.when(step == pl.num_programs(0) - 1)
    def _():
        for p in range(3):
            for r in range(PATCH):
                units_ref[
                    p * PLANE_TOKENS : (p + 1) * PLANE_TOKENS, r * CELLS : (r + 1) * CELLS
                ] = grad_ref[p, r * PLANE_TOKENS : (r + 1) * PLANE_TOKENS, :].astype(BF16)
        gtok_ref[...] = dot(units_ref[...], w_ref[...], NT)


def scene_pass(tokens, w_unpatch, spots, edges, cot, own, small, slab_edges):
    dens_in, dens_bias, dens_out, color_in, color_bias, color_out = small
    net = jnp.concatenate(
        [
            dens_in,
            color_in,
            jnp.pad(color_out.T, ((0, 0), (0, 8 - color_out.shape[0]))),
            dens_bias[:, None],
            dens_out[:, None],
            color_bias[:, None],
        ],
        axis=1,
    )
    net = jnp.pad(net, ((0, 0), (0, 128 - net.shape[1])))
    total = spots.shape[1]
    block = min(512, slab_edges)
    const = lambda shape: pl.BlockSpec(shape, lambda i, own: (0,) * len(shape))
    lanes = lambda rows: pl.BlockSpec((rows, block), lambda i, own: (0, i))
    dens, colr = dens_in.shape[0], color_in.shape[0]
    outs = [
        ((8, total), F32, lanes(8)),
        ((TRI, w_unpatch.shape[1]), BF16, None),
        ((TRI, w_unpatch.shape[0]), F32, None),
        ((dens, FEAT), F32, None),
        ((dens, 1), F32, None),
        ((dens, 1), F32, None),
        ((colr, FEAT), F32, None),
        ((colr, 1), F32, None),
        ((8, colr), F32, None),
    ]
    return pl.pallas_call(
        functools.partial(scene_kernel, per_slab=slab_edges // block),
        grid_spec=pltpu.PrefetchScalarGridSpec(
            num_scalar_prefetch=1,
            grid=(total // block,),
            in_specs=[
                const(tokens.shape),
                const(w_unpatch.shape),
                lanes(16),
                lanes(8),
                lanes(8),
                const((dens, 128)),
            ],
            out_specs=[s if s is not None else const(shape) for shape, _, s in outs],
            scratch_shapes=[
                pltpu.VMEM((3, 2 * CELLS, SPOTS), BF16),
                pltpu.VMEM((3, SPOTS, 2 * block), BF16),
                pltpu.VMEM((3, SPOTS, CELLS), F32),
            ],
        ),
        out_shape=[jax.ShapeDtypeStruct(shape, kind) for shape, kind, _ in outs],
        compiler_params=pltpu.CompilerParams(vmem_limit_bytes=56 * 1024 * 1024),
        cost_estimate=cost(25e9, 8 * w_unpatch.size, 1e6),
        name="scene",
    )(
        own,
        tokens,
        w_unpatch,
        spots,
        edges,
        cot,
        net,
    )


def edge_tables(edge_rows, blend_rows, live_counts, slab_planes):
    slabs, count = edge_rows.shape
    plane_cells = GRID * GRID
    slab_cells = slab_planes * plane_cells
    direction = edge_rows // slab_cells
    cell = edge_rows % slab_cells
    first = (jnp.arange(slabs, dtype=jnp.int32) * slab_planes)[:, None]
    i_a = cell // plane_cells + first
    j_a = (cell % plane_cells) // GRID
    l_a = cell % GRID
    i_b = i_a + (direction == 0)
    j_b = j_a + (direction == 1)
    l_b = l_a + (direction == 2)
    valid = (j_b < GRID) & (l_b < GRID)
    inside = valid & (i_b < GRID)

    def place(row, col, keep):
        spot = (row % PATCH) * PLANE_TOKENS + (row // PATCH) * SIDE + col // PATCH
        return jnp.where(keep, spot, -1), col % PATCH

    on = jnp.ones_like(valid)
    pairs = [
        place(i_a, j_a, on),
        place(i_a, l_a, on),
        place(j_a, l_a, on),
        place(i_b, j_b, inside),
        place(i_b, l_b, inside),
        place(j_b, l_b, inside),
    ]
    blank_i = jnp.zeros_like(edge_rows)
    spots = jnp.stack([a for a, _ in pairs] + [b for _, b in pairs] + [blank_i] * 4)
    w_b = blend_rows.astype(F32) / 16.0
    w_a = 1.0 - w_b
    live = jnp.arange(count, dtype=jnp.int32)[None, :] < live_counts
    blank = jnp.zeros_like(w_b)
    edges = jnp.stack(
        [w_a, w_b * valid.astype(F32), inside.astype(F32), live.astype(F32)] + [blank] * 4
    )
    return spots.reshape(16, slabs * count), edges.reshape(8, slabs * count)


def swap(x, axis="tp"):
    return lax.ppermute(x, axis, [(0, 1), (1, 0)])


def tp_sum(partial, *gates):
    if lax.axis_size("tp") == 2:
        return partial.astype(F32) + after(swap(partial), *gates).astype(F32)
    return lax.psum(partial.astype(F32), "tp")


def tp_parts(partial):
    count = lax.axis_size("tp")
    if count != 2:
        return partial, partial
    rows = partial.shape[0] // count
    me = lax.axis_index("tp")
    theirs = lax.dynamic_slice_in_dim(partial, (1 - me) * rows, rows, 0).astype(BF16)
    return lax.dynamic_slice_in_dim(partial, me * rows, rows, 0), theirs


def tp_sum_own(mine, theirs, *gates):
    if lax.axis_size("tp") == 2:
        return mine + after(swap(theirs), *gates).astype(F32)
    return lax.psum_scatter(mine, "tp", scatter_dimension=0, tiled=True)


def tp_rows(own):
    if lax.axis_size("tp") == 2:
        other = swap(own)
        first = lax.axis_index("tp") == 0
        return jnp.concatenate(
            [jnp.where(first, own, other), jnp.where(first, other, own)], axis=0
        )
    return lax.all_gather(own, "tp", axis=0, tiled=True)


LINE, WIDE, CORES = 4, 2, 2


def blocks_known():
    return lax.axis_size("seq") == LINE * WIDE * CORES


def own_places(blocks):
    block = jnp.arange(blocks, dtype=jnp.int32)
    if not blocks_known():
        return block
    me = lax.axis_index("seq")
    w, c = (me // CORES) % WIDE, me % CORES
    z, x, core = block // (WIDE * CORES), (block // CORES) % WIDE, block % CORES
    return ((core ^ c) * WIDE + (x ^ w)) * LINE + z


def hop(x, kind):
    pairs = []
    for i in range(LINE * WIDE * CORES):
        z, w, c = i // (WIDE * CORES), (i // CORES) % WIDE, i % CORES
        if kind == "core":
            c = 1 - c
        else:
            w = 1 - w
        pairs.append((i, (z * WIDE + w) * CORES + c))
    return lax.ppermute(x, "seq", pairs)


def along_line(x):
    step = WIDE * CORES
    groups = [[z * step + i for z in range(LINE)] for i in range(step)]
    return lax.all_to_all(x, "seq", 0, 0, axis_index_groups=groups, tiled=True)


def gather_plain(shard):
    return lax.all_gather(shard, "seq", axis=0, tiled=True)


def scatter_plain(grad):
    return lax.psum_scatter(grad, "seq", scatter_dimension=0, tiled=True)


def gather_line(shard):
    return along_line(jnp.concatenate([shard] * LINE, 0))


def assemble_kernel(place_ref, *refs):
    *parts, out_ref = refs
    for i, part in enumerate(parts):
        rows = part.shape[0]
        out_ref[pl.ds(pl.multiple_of(place_ref[i] * rows, rows), rows), :] = part[...]


def gather_rest(line, wide):
    me = lax.axis_index("seq")
    w, c = (me // CORES) % WIDE, me % CORES
    parts = [line, wide, hop(line, "core"), hop(wide, "core")]
    place = [(w ^ xr) * CORES + (c ^ cr) for cr in range(CORES) for xr in range(WIDE)]
    rows, width = line.shape[0] // LINE, line.shape[1]
    return pl.pallas_call(
        assemble_kernel,
        grid_spec=pltpu.PrefetchScalarGridSpec(
            num_scalar_prefetch=1,
            grid=(LINE,),
            in_specs=[pl.BlockSpec((rows, width), lambda i, place: (i, 0))] * len(parts),
            out_specs=pl.BlockSpec((len(parts) * rows, width), lambda i, place: (i, 0)),
        ),
        out_shape=jax.ShapeDtypeStruct((len(parts) * line.shape[0], width), line.dtype),
        cost_estimate=cost(0, 16 * line.size),
        compiler_params=pltpu.CompilerParams(vmem_limit_bytes=24 * 1024 * 1024),
        name="assemble",
    )(jnp.stack(place).astype(jnp.int32), *parts)


def add_rounded(a, b):
    return (a.astype(F32) + b.astype(F32)).astype(BF16)


def scatter_chip(near, far):
    if not blocks_known():
        return jnp.concatenate([near, far], 0)
    return add_rounded(near, hop(far, "core"))


def scatter_pair(chip):
    if not blocks_known():
        return chip
    half = chip.shape[0] // WIDE
    return add_rounded(chip[:half], hop(chip[half:], "x"))


def scatter_line(pair):
    if not blocks_known():
        return lax.psum_scatter(pair, "seq", scatter_dimension=0, tiled=True).astype(F32)
    parts = along_line(pair).reshape(LINE, -1, pair.shape[1])
    return jnp.sum(parts.astype(F32), axis=0)


def sum_by_hops(vec):
    for axis, steps in (("seq", (4, 8)), ("tp", (1,)), ("seq", (1, 2))):
        size = lax.axis_size(axis)
        if axis == "tp" and size > 2:
            steps = tuple(2**i for i in range(size.bit_length() - 1))
        if steps == (4, 8) and size > 16:
            steps = tuple(2**i for i in range(2, size.bit_length() - 1))
        for step in steps:
            vec = vec + lax.ppermute(vec, axis, [(i, i ^ step) for i in range(size)])
    return vec


def shards(
    layer_input,
    attn_gain,
    w_qkv,
    w_out,
    mlp_gain,
    w_up,
    w_down,
    w_unpatch,
    dens_in,
    dens_bias,
    dens_out,
    color_in,
    color_bias,
    color_out,
    edge_ids,
    blend_steps,
    live_count,
    color_grad,
    out_grad,
):
    tp_count = lax.axis_size("tp")
    tp_index = lax.axis_index("tp")
    length, model_width = layer_input.shape
    own_rows = length // tp_count
    own_tri = TRI // tp_count
    own_rest = own_rows - own_tri
    slab_planes = GRID // tp_count
    slab_edges = edge_ids.shape[1]

    def split_rows(x):
        blocks = x.reshape(tp_count, own_rows, x.shape[-1])
        return (
            blocks[:, own_rest:].reshape(TRI, x.shape[-1]),
            blocks[:, :own_rest].reshape(length - TRI, x.shape[-1]),
        )

    def block_rows(x):
        tri = x[:TRI].reshape(tp_count, own_tri, x.shape[-1])
        rest = x[TRI:].reshape(tp_count, own_rest, x.shape[-1])
        return jnp.concatenate([rest, tri], 1).reshape(length, x.shape[-1])

    def own_columns(x, width):
        if width == x.shape[1]:
            return x
        return lax.dynamic_slice_in_dim(x, tp_index * width, width, 1)

    def own_of(rows, count):
        return lax.dynamic_slice_in_dim(rows, tp_index * count, count, 0)

    packed = jnp.concatenate(
        [
            edge_ids.astype(F32),
            blend_steps.astype(F32),
            jnp.broadcast_to(live_count.astype(F32), edge_ids.shape),
            color_grad[:, 0],
        ],
        0,
    )
    slabs = tp_rows(packed).reshape(tp_count, packed.shape[0], slab_edges)
    spots, edges = edge_tables(
        slabs[:, 0].astype(jnp.int32), slabs[:, 1], slabs[:, 2, :1].astype(jnp.int32), slab_planes
    )
    cot = slabs[:, 3:].swapaxes(0, 1).reshape(-1, tp_count * slab_edges)
    cot = jnp.pad(cot, ((0, 8 - cot.shape[0]), (0, 0)))

    places = own_places(model_width // 64)
    in_order = jnp.arange(model_width // 64, dtype=jnp.int32)
    x_tri, x_rest = split_rows(layer_input)
    rows_in = jnp.concatenate([x_tri, x_rest], 0)
    og_tri, og_rest = split_rows(out_grad)
    gm_rest = og_rest.astype(BF16)
    og_own = own_of(og_rest, own_rest)

    local_width = w_out.shape[0]
    first = gather_plain(jnp.concatenate([w_qkv.reshape(w_qkv.shape[0], -1), w_out.T], 1))
    first = after(first, spots, edges, cot, gm_rest, rows_in)
    if blocks_known():
        line_u = gather_line(w_up)
        first = after(first, line_u)
    else:
        line_u = w_up
    down_t = gather_plain(after(w_down.T, first))
    qkv_full, out_t = first[:, : 3 * local_width], first[:, 3 * local_width :]

    normed_a = layer_norm(rows_in.astype(F32), attn_gain).astype(BF16)
    projected = dot(normed_a, qkv_full).astype(BF16)
    attended, lse = attend_fwd(projected, local_width)
    if blocks_known():
        wide_u = hop(line_u, "x")
        up_full = gather_rest(line_u, wide_u)
    else:
        wide_u = line_u
        up_full = gather_plain(w_up)
    rest_own = own_of(x_rest, own_rest).astype(F32)
    out_tri = dot(attended[:TRI], out_t, NT)
    mine, theirs = tp_parts(dot(after(attended, out_tri)[TRI:], out_t, NT))
    hidden_tri = x_tri.astype(F32) + tp_sum(out_tri, theirs)
    hidden_rest = rest_own + tp_sum_own(mine, theirs)

    normed_own = layer_norm(hidden_rest, mlp_gain).astype(BF16)
    unpatch_full = gather_plain(after(w_unpatch, hidden_tri, normed_own, wide_u))

    normed_tri = layer_norm(hidden_tri, mlp_gain).astype(BF16)
    tokens = (hidden_tri + tp_sum(mlp_tri(normed_tri, up_full, down_t).astype(BF16))).astype(BF16)
    normed_rest = tp_rows(normed_own)

    act_rest, gup_rest = mlp_mid(after(normed_rest, tokens), gm_rest, up_full, down_t)
    gnb_mine, gnb_theirs = tp_parts(dot(gup_rest, up_full, NT))
    tokens = after(tokens, gnb_theirs)

    (
        colors_all,
        grad_units,
        grad_tokens,
        g_dens_in,
        g_dens_bias,
        g_dens_out,
        g_color_in,
        g_color_bias,
        g_color_out,
    ) = scene_pass(
        tokens,
        unpatch_full,
        spots,
        edges,
        cot,
        tp_index[None].astype(jnp.int32),
        (dens_in, dens_bias, dens_out, color_in, color_bias, color_out),
        slab_edges,
    )
    colors = lax.dynamic_slice_in_dim(
        colors_all[: color_out.shape[0]], tp_index * slab_edges, slab_edges, 1
    )
    gnb_rest = tp_sum_own(gnb_mine, gnb_theirs, grad_tokens)
    go_tri = og_tri + grad_tokens
    gm_tri = go_tri.astype(BF16)
    act_tri, gup_tri = mlp_mid(normed_tri, gm_tri, up_full, down_t)
    gnb_tri = tp_sum(dot(gup_tri, up_full, NT).astype(BF16))
    grad_down = weight_grad(in_order, 1, ((gm_rest, gm_tri), (act_rest, act_tri)))[0]
    sum_down = scatter_plain(grad_down).astype(F32)
    width = grad_units.shape[1] // tp_count if tp_count == 2 else grad_units.shape[1]
    sum_unpatch = scatter_plain(dot(tokens, own_columns(grad_units, width), TN).astype(BF16))
    grad_up = weight_grad(places, 2, ((normed_rest, normed_tri), (gup_rest, gup_tri)))
    _, back_rest = jax.vjp(layer_norm, hidden_rest, mlp_gain)
    gh_rest, gain_rest = back_rest(gnb_rest)
    _, back_tri = jax.vjp(lambda h: layer_norm(h, mlp_gain), hidden_tri)
    gh_tri = back_tri(gnb_tri)[0] + go_tri
    _, back_gain = jax.vjp(lambda g: layer_norm(own_of(hidden_tri, own_tri), g), mlp_gain)
    grad_mlp_gain = gain_rest + back_gain(own_of(gnb_tri, own_tri))[0]
    gh_rest = gh_rest + og_own
    branch = jnp.concatenate([gh_tri.astype(BF16), tp_rows(gh_rest.astype(BF16))], 0)

    smalls = (
        grad_mlp_gain,
        g_dens_in,
        g_dens_bias,
        g_dens_out,
        g_color_in,
        g_color_bias,
        g_color_out[: color_out.shape[0]],
    )
    flat = sum_by_hops(jnp.concatenate([s.reshape(-1) for s in smalls]))

    chip_up = scatter_chip(*grad_up)
    grad_heads = dot(branch, out_t).astype(BF16)
    grad_heads = after(grad_heads, chip_up, grad_down, flat)
    pair_up = scatter_pair(chip_up)
    grad_proj = attend_bwd(projected, grad_heads, attended, lse, local_width)
    grad_proj = after(grad_proj, pair_up)
    sum_up = scatter_line(pair_up)
    gna = dot(grad_proj, qkv_full, NT)
    gna_sum = tp_sum_own(*tp_parts(block_rows(gna)))
    chip_last = scatter_chip(
        *weight_grad(places, 2, ((normed_a,), (grad_proj,)), ((branch,), (attended,)))
    )
    pair_last = scatter_pair(chip_last)
    sum_last = scatter_line(after(pair_last, gna_sum))
    _, back_gain_a = jax.vjp(lambda g: layer_norm(rows_in.astype(F32), g), attn_gain)
    grad_attn_gain = back_gain_a(gna)[0]
    tri_own = own_of(x_tri, own_tri).astype(F32)
    _, back_a = jax.vjp(
        lambda v: layer_norm(v, attn_gain), jnp.concatenate([rest_own, tri_own], 0)
    )
    grad_input = back_a(gna_sum)[0] + jnp.concatenate(
        [gh_rest, own_of(gh_tri, own_tri)], 0
    )
    if tp_count == 2:
        other = swap(sum_unpatch)
        low = tp_index == 0
        sum_unpatch = jnp.concatenate(
            [jnp.where(low, sum_unpatch, other), jnp.where(low, other, sum_unpatch)], 1
        )
    sum_unpatch = sum_unpatch.astype(F32)

    weight_sums = (
        sum_last[:, : 3 * local_width].reshape(w_qkv.shape),
        sum_last[:, 3 * local_width :].T,
        sum_up,
        sum_down.T,
        sum_unpatch,
    )
    small_sums = [sum_by_hops(after(grad_attn_gain, pair_last))]
    at = 0
    for s in smalls:
        small_sums.append(flat[at : at + s.size].reshape(s.shape))
        at += s.size
    for i in (3, 4, 6):
        small_sums[i] = small_sums[i].reshape(-1)
    return (
        colors[:, None, :],
        grad_input,
        small_sums[0],
        weight_sums[0],
        weight_sums[1],
        small_sums[1],
        weight_sums[2],
        weight_sums[3],
        weight_sums[4],
        small_sums[2],
        small_sums[3],
        small_sums[4],
        small_sums[5],
        small_sums[6],
        small_sums[7],
    )


def solution(mesh):
    placed = (
        P("seq", None),
        P(),
        P("seq", None, "tp"),
        P("tp", "seq"),
        P(),
        P("seq", "tp"),
        P("tp", "seq"),
        P("seq", None),
        P(),
        P(),
        P(),
        P(),
        P(),
        P(),
        P("seq", "tp"),
        P("seq", "tp"),
        P("seq", "tp"),
        P(None, "seq", "tp"),
        P("seq", None),
    )
    return jax.shard_map(
        shards,
        mesh=mesh,
        in_specs=placed,
        out_specs=(
            P(None, "seq", "tp"),
            P(("seq", "tp"), None),
            P(),
            P("seq", None, "tp"),
            P("tp", "seq"),
            P(),
            P("seq", "tp"),
            P("tp", "seq"),
            P("seq", None),
            P(),
            P(),
            P(),
            P(),
            P(),
            P(),
        ),
        check_vma=False,
    )
```

```python
import functools
import math

import jax
import jax.numpy as jnp
from jax import lax
from jax.experimental import pallas as pl
from jax.experimental.pallas import tpu as pltpu
from jax.sharding import PartitionSpec as P

HEAD_DIM = 64
FEAT = 32
PATCH = 8
GRID = 64
TRI = 192
SIDE = GRID // PATCH
PLANE_TOKENS = SIDE * SIDE
SPOTS = PLANE_TOKENS * PATCH
CELLS = PATCH * FEAT

HIGHEST = lax.Precision.HIGHEST
BF16 = jnp.bfloat16
F32 = jnp.float32
NN = (((1,), (0,)), ((), ()))
NT = (((1,), (1,)), ((), ()))
TN = (((0,), (0,)), ((), ()))


def cost(flops, moved, exps=0):
    return pl.CostEstimate(flops=int(flops), bytes_accessed=int(moved), transcendentals=int(exps))


def dot(a, b, dims=NN, precision=None):
    return lax.dot_general(a, b, dims, precision=precision, preferred_element_type=F32)


def gelu_parts(x):
    density = jnp.exp(-0.5 * x * x)
    t = 1.0 / (1.0 + (0.3275911 * 2.0**-0.5) * jnp.abs(x))
    poly = ((((1.061405429 * t - 1.453152027) * t + 1.421413741) * t - 0.284496736) * t + 0.254829592) * t
    tail = 0.5 * poly * density
    cdf = jnp.where(x < 0.0, tail, 1.0 - tail)
    return x * cdf, cdf + x * (density * (1.0 / math.sqrt(2.0 * math.pi)))


def leave(*refs):
    pass


def after(x, *others):
    if not others:
        return x
    anywhere = pl.BlockSpec(memory_space=pl.ANY)
    return pl.pallas_call(
        leave,
        in_specs=[anywhere] * (1 + len(others)),
        out_specs=anywhere,
        out_shape=jax.ShapeDtypeStruct(x.shape, x.dtype),
        input_output_aliases={0: 0},
        name="after",
    )(x, *others)


def layer_norm(values, gain_vec):
    center = values - jnp.mean(values, axis=-1, keepdims=True)
    spread = jnp.mean(center * center, axis=-1, keepdims=True)
    return center * lax.rsqrt(spread + 1e-05) * gain_vec


def attend_fwd_kernel(q_ref, k_ref, v_ref, o_ref, lse_ref, *, scale, block):
    length, width = q_ref.shape
    heads = width // HEAD_DIM
    lane = lax.broadcasted_iota(jnp.int32, (1, width), 1) // HEAD_DIM
    lane_block = lax.broadcasted_iota(jnp.int32, (block, width), 1)
    keys = k_ref[...]
    values = v_ref[...]
    zero = jnp.zeros((), BF16)
    masked = [jnp.where(lane == h, keys, zero) for h in range(heads)]
    for b in range(length // block):
        rows = pl.ds(b * block, block)
        q = (q_ref[rows, :].astype(F32) * scale).astype(BF16)
        result = jnp.zeros((block, width), F32)
        stats = jnp.zeros((block, width), F32)
        for h in range(heads):
            s = dot(q, masked[h], NT)
            top = jnp.max(s, axis=1, keepdims=True)
            p = jnp.exp(s - top)
            total = jnp.sum(p, axis=1, keepdims=True)
            o = dot((p * (1.0 / total)).astype(BF16), values)
            result = jnp.where(lane == h, o, result)
            stats = jnp.where(lane_block == h, top + jnp.log(total), stats)
        o_ref[rows, :] = result.astype(BF16)
        lse_ref[0, :, pl.ds(b * block, block)] = stats.T[:8, :]


def attend_fwd(projected, local_width):
    length = projected.shape[0]
    width = 2 * HEAD_DIM
    pairs = local_width // width
    spec = lambda part: pl.BlockSpec((length, width), lambda i: (0, part * pairs + i))
    return pl.pallas_call(
        functools.partial(attend_fwd_kernel, scale=HEAD_DIM**-0.5, block=512),
        grid=(pairs,),
        in_specs=[spec(0), spec(1), spec(2)],
        out_specs=[
            pl.BlockSpec((length, width), lambda i: (0, i)),
            pl.BlockSpec((1, 8, length), lambda i: (i, 0, 0)),
        ],
        out_shape=[
            jax.ShapeDtypeStruct((length, local_width), BF16),
            jax.ShapeDtypeStruct((pairs, 8, length), F32),
        ],
        compiler_params=pltpu.CompilerParams(vmem_limit_bytes=48 * 1024 * 1024),
        cost_estimate=cost(
            12 * length * length * local_width, 8 * length * local_width, length * length * pairs * 2
        ),
        name="attend_fwd",
    )(projected, projected, projected)


def attend_bwd_kernel(
    q_ref, k_ref, v_ref, g_ref, o_ref, lse_ref, out_ref, dq_ref, dk_ref, dv_ref, *, scale, block
):
    length, width = q_ref.shape
    heads = width // HEAD_DIM
    step = pl.program_id(1)

    @pl.when(step == 0)
    def _():
        lane = lax.broadcasted_iota(jnp.int32, (1, width), 1) // HEAD_DIM
        keys = k_ref[...]
        values = v_ref[...]
        zero = jnp.zeros((), BF16)
        key_cols = keys.T
        prod = g_ref[...].astype(F32) * o_ref[...].astype(F32)
        pick = (
            lax.broadcasted_iota(jnp.int32, (8, width), 1) // HEAD_DIM
            == lax.broadcasted_iota(jnp.int32, (8, width), 0)
        ).astype(F32)
        inner = dot(pick, prod, NT, HIGHEST)
        for h in range(heads):
            k_h = jnp.where(lane == h, keys, zero)
            v_h = jnp.where(lane == h, values, zero)
            for b in range(length // block):
                rows = pl.ds(b * block, block)
                q = (q_ref[rows, :].astype(F32) * scale).astype(BF16)
                g = g_ref[rows, :]
                s = dot(k_h, q, NT)
                p = jnp.exp(s - lse_ref[0, h : h + 1, b * block : (b + 1) * block])
                dp = dot(v_h, g, NT)
                ds = (p * (dp - inner[h : h + 1, b * block : (b + 1) * block])).astype(BF16)
                dv = dot(p.astype(BF16), jnp.where(lane == h, g, zero))
                dk = dot(ds, jnp.where(lane == h, q, zero))
                if h == 0 and b == 0:
                    dv_ref[...] = dv
                    dk_ref[...] = dk
                else:
                    dv_ref[...] += dv
                    dk_ref[...] += dk
                dq_ref[h * HEAD_DIM : (h + 1) * HEAD_DIM, b * block : (b + 1) * block] = (
                    dot(key_cols[h * HEAD_DIM : (h + 1) * HEAD_DIM, :], ds) * scale
                )
        out_ref[...] = dq_ref[...].T.astype(BF16)

    @pl.when(step == 1)
    def _():
        out_ref[...] = dk_ref[...].astype(BF16)

    @pl.when(step == 2)
    def _():
        out_ref[...] = dv_ref[...].astype(BF16)


def attend_bwd(projected, grad_heads, attended, lse, local_width):
    length = projected.shape[0]
    width = 2 * HEAD_DIM
    pairs = local_width // width
    spec = lambda part: pl.BlockSpec((length, width), lambda i, j: (0, part * pairs + i))
    return pl.pallas_call(
        functools.partial(attend_bwd_kernel, scale=HEAD_DIM**-0.5, block=256),
        grid=(pairs, 3),
        in_specs=[
            spec(0),
            spec(1),
            spec(2),
            spec(0),
            spec(0),
            pl.BlockSpec((1, 8, length), lambda i, j: (i, 0, 0)),
        ],
        out_specs=pl.BlockSpec((length, width), lambda i, j: (0, j * pairs + i)),
        out_shape=jax.ShapeDtypeStruct((length, 3 * local_width), BF16),
        scratch_shapes=[
            pltpu.VMEM((width, length), F32),
            pltpu.VMEM((length, width), F32),
            pltpu.VMEM((length, width), F32),
        ],
        compiler_params=pltpu.CompilerParams(vmem_limit_bytes=48 * 1024 * 1024),
        cost_estimate=cost(
            24 * length * length * local_width, 16 * length * local_width, length * length * pairs * 2
        ),
        name="attend_bwd",
    )(projected, projected, projected, grad_heads, attended, lse)


def mlp_mid_kernel(nb_ref, gm_ref, up_ref, down_ref, act_ref, gup_ref, *, block):
    up = up_ref[...]
    down = down_ref[...]
    for b in range(nb_ref.shape[0] // block):
        rows = pl.ds(b * block, block)
        value, slope = gelu_parts(dot(nb_ref[rows, :], up))
        act_ref[rows, :] = value.astype(BF16)
        gup_ref[rows, :] = (slope * dot(gm_ref[rows, :], down)).astype(BF16)


def mlp_mid(normed, grad, up_full, down_full):
    rows, depth = normed.shape
    width = up_full.shape[1]
    cols = min(width, 512)
    block = rows
    for cand in (416, 192):
        if rows % cand == 0:
            block = cand
            break
    whole = pl.BlockSpec((rows, depth), lambda i: (0, 0))
    weight = pl.BlockSpec((depth, cols), lambda i: (0, i))
    result = pl.BlockSpec((rows, cols), lambda i: (0, i))
    return pl.pallas_call(
        functools.partial(mlp_mid_kernel, block=block),
        grid=(width // cols,),
        in_specs=[whole, whole, weight, weight],
        out_specs=[result, result],
        out_shape=[jax.ShapeDtypeStruct((rows, width), BF16)] * 2,
        compiler_params=pltpu.CompilerParams(vmem_limit_bytes=60 * 1024 * 1024),
        cost_estimate=cost(
            8 * rows * depth * width, 4 * (rows + width) * depth + 4 * rows * width, rows * width
        ),
        name="mlp_mid",
    )(normed, grad, up_full, down_full)


def mlp_tri_kernel(nb_ref, up_ref, down_ref, out_ref):
    value, _ = gelu_parts(dot(nb_ref[...], up_ref[...]))
    part = dot(value.astype(BF16), down_ref[...], NT)

    @pl.when(pl.program_id(0) == 0)
    def _():
        out_ref[...] = part

    @pl.when(pl.program_id(0) > 0)
    def _():
        out_ref[...] += part


def mlp_tri(normed, up_full, down_full):
    rows, depth = normed.shape
    width = up_full.shape[1]
    cols = min(width, 512)
    whole = pl.BlockSpec((rows, depth), lambda i: (0, 0))
    weight = pl.BlockSpec((depth, cols), lambda i: (0, i))
    return pl.pallas_call(
        mlp_tri_kernel,
        grid=(width // cols,),
        in_specs=[whole, weight, weight],
        out_specs=whole,
        out_shape=jax.ShapeDtypeStruct((rows, depth), F32),
        compiler_params=pltpu.CompilerParams(vmem_limit_bytes=60 * 1024 * 1024),
        cost_estimate=cost(4e9, 4 * width * depth, rows * width),
        name="mlp_tri",
    )(normed, up_full, down_full)


def weight_grad_kernel(place_ref, *refs, segments, pieces):
    step = pl.program_id(0)
    rest = refs[2 * sum(n for n, _, _ in segments) :]
    outs, turned = rest[:pieces], rest[pieces:]
    at = 0
    for parts, first, last in segments:
        lefts, rights = refs[at : at + parts], refs[at + parts : at + 2 * parts]
        at += 2 * parts

        @pl.when(step == first)
        def _():
            for left, spot in zip(lefts, turned):
                rows = left.shape[0]
                for j in range(left.shape[1] // 128):
                    both = left[:, j * 128 : (j + 1) * 128].T
                    for k in range(2):
                        to = pl.multiple_of(place_ref[2 * j + k] * 64, 64)
                        spot[pl.ds(to, 64), :rows] = both[k * 64 : (k + 1) * 64]

        @pl.when((step >= first) & (step <= last))
        def _():
            total = sum(
                dot(spot[:, : right.shape[0]], right[...]) for spot, right in zip(turned, rights)
            )
            for i, out in enumerate(outs):
                rows = out.shape[0]
                out[...] = total[i * rows : (i + 1) * rows].astype(BF16)


def weight_grad(place, pieces, *segments, room=40):
    specs, args, marks = [], [], []
    first = 0
    cols = min(512, *(rights[0].shape[1] for _, rights in segments))
    depth = segments[0][0][0].shape[1]
    for lefts, rights in segments:
        steps = rights[0].shape[1] // cols
        for left in lefts:
            specs.append(pl.BlockSpec(left.shape, lambda i, place: (0, 0)))
            args.append(left)
        for right in rights:
            specs.append(
                pl.BlockSpec(
                    (right.shape[0], cols),
                    lambda i, place, a=first, b=steps: (0, jnp.clip(i - a, 0, b - 1)),
                )
            )
            args.append(right)
        marks.append((len(lefts), first, first + steps - 1))
        first += steps
    parts = segments[0][0]
    result = jax.ShapeDtypeStruct((depth // pieces, first * cols), BF16)
    return pl.pallas_call(
        functools.partial(weight_grad_kernel, segments=tuple(marks), pieces=pieces),
        grid_spec=pltpu.PrefetchScalarGridSpec(
            num_scalar_prefetch=1,
            grid=(first,),
            in_specs=specs,
            out_specs=[pl.BlockSpec((depth // pieces, cols), lambda i, place: (0, i))] * pieces,
            scratch_shapes=[pltpu.VMEM((depth, left.shape[0]), BF16) for left in parts],
        ),
        out_shape=[result] * pieces,
        compiler_params=pltpu.CompilerParams(vmem_limit_bytes=room * 1024 * 1024),
        cost_estimate=cost(
            3 * depth * first * cols * sum(left.shape[0] for left in parts), 8 * depth * first * cols
        ),
        name="weight_grad",
    )(place, *args)


def split_halves(x):
    high = x.astype(BF16)
    return high, (x - high.astype(F32)).astype(BF16)


def dot_fine(a, b):
    a_high, a_low = split_halves(a)
    b_high, b_low = split_halves(b)
    return dot(
        jnp.concatenate([a_high, a_high, a_low], axis=1),
        jnp.concatenate([b_high, b_low, b_high], axis=0),
    )


def dot_fine_lanes(a, b):
    rows, cols = a.shape[0], b.shape[0]
    both = dot(
        jnp.concatenate(split_halves(a), axis=0), jnp.concatenate(split_halves(b), axis=0), NT
    )
    return both[:rows, :cols] + both[:rows, cols:] + both[rows:, :cols]


def scene_kernel(
    own_ref,
    tokens_ref,
    w_ref,
    spot_ref,
    edge_ref,
    cot_ref,
    net_ref,
    colors_ref,
    units_ref,
    gtok_ref,
    gdi_ref,
    gdb_ref,
    gdo_ref,
    gci_ref,
    gcb_ref,
    gco_ref,
    table_ref,
    hot_ref,
    grad_ref,
    *,
    per_slab,
):
    step = pl.program_id(0)
    block = spot_ref.shape[1]
    ends = 2 * block

    @pl.when(step == 0)
    def _():
        units = dot(tokens_ref[...], w_ref[...])
        for p in range(3):
            rows = jnp.concatenate(
                [
                    units[p * PLANE_TOKENS : (p + 1) * PLANE_TOKENS, r * CELLS : (r + 1) * CELLS]
                    for r in range(PATCH)
                ],
                axis=0,
            )
            high, low = split_halves(rows.T)
            table_ref[p, :CELLS, :] = high
            table_ref[p, CELLS:, :] = low
        grad_ref[...] = jnp.zeros_like(grad_ref)
        for ref in (gdi_ref, gdb_ref, gdo_ref, gci_ref, gcb_ref, gco_ref):
            ref[...] = jnp.zeros_like(ref)

    net = net_ref[...]
    dens_in, color_in = net[:, :FEAT], net[:, FEAT : 2 * FEAT]
    color_out_t = net[:, 2 * FEAT : 2 * FEAT + 8]
    at = 2 * FEAT + 8
    dens_bias, dens_out, color_bias = net[:, at : at + 1], net[:, at + 1 : at + 2], net[:, at + 2 : at + 3]
    dens_in_t, color_in_t, color_out = dens_in.T, color_in.T, color_out_t.T
    iota = lax.broadcasted_iota(jnp.int32, (SPOTS, ends), 0)
    field = jnp.zeros((FEAT, ends), F32)
    columns = []
    for p in range(3):
        spot = jnp.concatenate([spot_ref[p : p + 1, :], spot_ref[3 + p : 4 + p, :]], axis=1)
        column = jnp.concatenate([spot_ref[6 + p : 7 + p, :], spot_ref[9 + p : 10 + p, :]], axis=1)
        columns.append(column)
        hot = jnp.where(iota == spot, 1.0, 0.0).astype(BF16)
        hot_ref[p] = hot
        found = dot(table_ref[p], hot)
        found = found[:CELLS] + found[CELLS:]
        for c in range(PATCH):
            field = field + jnp.where(column == c, found[c * FEAT : (c + 1) * FEAT], 0.0)

    w_a = edge_ref[0:1, :]
    w_b = edge_ref[1:2, :]
    inside = edge_ref[2:3, :]
    live = edge_ref[3:4, :]
    pre_d = dot_fine(dens_in, field) + dens_bias
    act_d, slope_d = gelu_parts(pre_d)
    dens = jnp.sum(act_d * dens_out, axis=0, keepdims=True)
    v_dens = w_a * dens[:, :block] + w_b * inside * dens[:, block:]
    v_feat = w_a * field[:, :block] + w_b * field[:, block:]
    pre_c = dot_fine(color_in, v_feat) + color_bias
    act_c, slope_c = gelu_parts(pre_c)
    shade = jax.nn.sigmoid(dot_fine(color_out, act_c))
    opacity = jax.nn.sigmoid(v_dens)
    colors_ref[...] = live * opacity * shade
    g_color = cot_ref[...] * live
    g_shade = g_color * opacity
    g_logit = g_shade * shade * (1.0 - shade)
    g_dens = jnp.sum(g_color * shade, axis=0, keepdims=True) * opacity * (1.0 - opacity)
    g_pre_c = dot_fine(color_out_t, g_logit) * slope_c
    g_feat = dot_fine(color_in_t, g_pre_c)
    g_dens2 = jnp.concatenate([w_a * g_dens, w_b * inside * g_dens], axis=1)
    g_pre_d = dens_out * g_dens2 * slope_d
    g_field = dot_fine(dens_in_t, g_pre_d) + jnp.concatenate(
        [w_a * g_feat, w_b * g_feat], axis=1
    )

    @pl.when(step // per_slab == own_ref[0])
    def _():
        gco_ref[...] += dot_fine_lanes(g_logit, act_c)
        gci_ref[...] += dot_fine_lanes(g_pre_c, v_feat)
        gcb_ref[...] += jnp.sum(g_pre_c, axis=1, keepdims=True)
        gdi_ref[...] += dot_fine_lanes(g_pre_d, field)
        gdb_ref[...] += jnp.sum(g_pre_d, axis=1, keepdims=True)
        gdo_ref[...] += jnp.sum(act_d * g_dens2, axis=1, keepdims=True)

    for p in range(3):
        spread = jnp.concatenate(
            [jnp.where(columns[p] == c, g_field, 0.0) for c in range(PATCH)], axis=0
        )
        grad_ref[p] += dot(hot_ref[p], spread.astype(BF16), NT)

    @pl.when(step == pl.num_programs(0) - 1)
    def _():
        for p in range(3):
            for r in range(PATCH):
                units_ref[
                    p * PLANE_TOKENS : (p + 1) * PLANE_TOKENS, r * CELLS : (r + 1) * CELLS
                ] = grad_ref[p, r * PLANE_TOKENS : (r + 1) * PLANE_TOKENS, :].astype(BF16)
        gtok_ref[...] = dot(units_ref[...], w_ref[...], NT)


def scene_pass(tokens, w_unpatch, spots, edges, cot, own, small, slab_edges):
    dens_in, dens_bias, dens_out, color_in, color_bias, color_out = small
    net = jnp.concatenate(
        [
            dens_in,
            color_in,
            jnp.pad(color_out.T, ((0, 0), (0, 8 - color_out.shape[0]))),
            dens_bias[:, None],
            dens_out[:, None],
            color_bias[:, None],
        ],
        axis=1,
    )
    net = jnp.pad(net, ((0, 0), (0, 128 - net.shape[1])))
    total = spots.shape[1]
    block = min(512, slab_edges)
    const = lambda shape: pl.BlockSpec(shape, lambda i, own: (0,) * len(shape))
    lanes = lambda rows: pl.BlockSpec((rows, block), lambda i, own: (0, i))
    dens, colr = dens_in.shape[0], color_in.shape[0]
    outs = [
        ((8, total), F32, lanes(8)),
        ((TRI, w_unpatch.shape[1]), BF16, None),
        ((TRI, w_unpatch.shape[0]), F32, None),
        ((dens, FEAT), F32, None),
        ((dens, 1), F32, None),
        ((dens, 1), F32, None),
        ((colr, FEAT), F32, None),
        ((colr, 1), F32, None),
        ((8, colr), F32, None),
    ]
    return pl.pallas_call(
        functools.partial(scene_kernel, per_slab=slab_edges // block),
        grid_spec=pltpu.PrefetchScalarGridSpec(
            num_scalar_prefetch=1,
            grid=(total // block,),
            in_specs=[
                const(tokens.shape),
                const(w_unpatch.shape),
                lanes(16),
                lanes(8),
                lanes(8),
                const((dens, 128)),
            ],
            out_specs=[s if s is not None else const(shape) for shape, _, s in outs],
            scratch_shapes=[
                pltpu.VMEM((3, 2 * CELLS, SPOTS), BF16),
                pltpu.VMEM((3, SPOTS, 2 * block), BF16),
                pltpu.VMEM((3, SPOTS, CELLS), F32),
            ],
        ),
        out_shape=[jax.ShapeDtypeStruct(shape, kind) for shape, kind, _ in outs],
        compiler_params=pltpu.CompilerParams(vmem_limit_bytes=60 * 1024 * 1024),
        cost_estimate=cost(25e9, 8 * w_unpatch.size, 1e6),
        name="scene",
    )(
        own,
        tokens,
        w_unpatch,
        spots,
        edges,
        cot,
        net,
    )


def edge_tables(edge_rows, blend_rows, live_counts, slab_planes):
    slabs, count = edge_rows.shape
    plane_cells = GRID * GRID
    slab_cells = slab_planes * plane_cells
    direction = edge_rows // slab_cells
    cell = edge_rows % slab_cells
    first = (jnp.arange(slabs, dtype=jnp.int32) * slab_planes)[:, None]
    i_a = cell // plane_cells + first
    j_a = (cell % plane_cells) // GRID
    l_a = cell % GRID
    i_b = i_a + (direction == 0)
    j_b = j_a + (direction == 1)
    l_b = l_a + (direction == 2)
    valid = (j_b < GRID) & (l_b < GRID)
    inside = valid & (i_b < GRID)

    def place(row, col, keep):
        spot = (row % PATCH) * PLANE_TOKENS + (row // PATCH) * SIDE + col // PATCH
        return jnp.where(keep, spot, -1), col % PATCH

    on = jnp.ones_like(valid)
    pairs = [
        place(i_a, j_a, on),
        place(i_a, l_a, on),
        place(j_a, l_a, on),
        place(i_b, j_b, inside),
        place(i_b, l_b, inside),
        place(j_b, l_b, inside),
    ]
    blank_i = jnp.zeros_like(edge_rows)
    spots = jnp.stack([a for a, _ in pairs] + [b for _, b in pairs] + [blank_i] * 4)
    w_b = blend_rows.astype(F32) / 16.0
    w_a = 1.0 - w_b
    live = jnp.arange(count, dtype=jnp.int32)[None, :] < live_counts
    blank = jnp.zeros_like(w_b)
    edges = jnp.stack(
        [w_a, w_b * valid.astype(F32), inside.astype(F32), live.astype(F32)] + [blank] * 4
    )
    return spots.reshape(16, slabs * count), edges.reshape(8, slabs * count)


def swap(x, axis="tp"):
    return lax.ppermute(x, axis, [(0, 1), (1, 0)])


def tp_sum(partial, *gates):
    if lax.axis_size("tp") == 2:
        return partial.astype(F32) + after(swap(partial), *gates).astype(F32)
    return lax.psum(partial.astype(F32), "tp")


def tp_parts(partial):
    count = lax.axis_size("tp")
    if count != 2:
        return partial, partial
    rows = partial.shape[0] // count
    me = lax.axis_index("tp")
    theirs = lax.dynamic_slice_in_dim(partial, (1 - me) * rows, rows, 0).astype(BF16)
    return lax.dynamic_slice_in_dim(partial, me * rows, rows, 0), theirs


def tp_sum_own(mine, theirs, *gates):
    if lax.axis_size("tp") == 2:
        return mine + after(swap(theirs), *gates).astype(F32)
    return lax.psum_scatter(mine, "tp", scatter_dimension=0, tiled=True)


def tp_rows(own):
    if lax.axis_size("tp") == 2:
        other = swap(own)
        first = lax.axis_index("tp") == 0
        return jnp.concatenate(
            [jnp.where(first, own, other), jnp.where(first, other, own)], axis=0
        )
    return lax.all_gather(own, "tp", axis=0, tiled=True)


LINE, WIDE, CORES = 4, 2, 2


def blocks_known():
    return lax.axis_size("seq") == LINE * WIDE * CORES


def own_places(blocks):
    block = jnp.arange(blocks, dtype=jnp.int32)
    if not blocks_known():
        return block
    me = lax.axis_index("seq")
    w, c = (me // CORES) % WIDE, me % CORES
    z, x, core = block // (WIDE * CORES), (block // CORES) % WIDE, block % CORES
    return ((core ^ c) * WIDE + (x ^ w)) * LINE + z


def hop(x, kind):
    pairs = []
    for i in range(LINE * WIDE * CORES):
        z, w, c = i // (WIDE * CORES), (i // CORES) % WIDE, i % CORES
        if kind == "core":
            c = 1 - c
        else:
            w = 1 - w
        pairs.append((i, (z * WIDE + w) * CORES + c))
    return lax.ppermute(x, "seq", pairs)


def along_line(x):
    step = WIDE * CORES
    groups = [[z * step + i for z in range(LINE)] for i in range(step)]
    return lax.all_to_all(x, "seq", 0, 0, axis_index_groups=groups, tiled=True)


def gather_plain(shard):
    return lax.all_gather(shard, "seq", axis=0, tiled=True)


def scatter_plain(grad):
    return lax.psum_scatter(grad, "seq", scatter_dimension=0, tiled=True)


def gather_line(shard):
    return along_line(jnp.concatenate([shard] * LINE, 0))


def assemble_kernel(place_ref, *refs):
    *parts, out_ref = refs
    for i, part in enumerate(parts):
        rows = part.shape[0]
        out_ref[pl.ds(pl.multiple_of(place_ref[i] * rows, rows), rows), :] = part[...]


def gather_rest(line, wide):
    me = lax.axis_index("seq")
    w, c = (me // CORES) % WIDE, me % CORES
    parts = [line, wide, hop(line, "core"), hop(wide, "core")]
    place = [(w ^ xr) * CORES + (c ^ cr) for cr in range(CORES) for xr in range(WIDE)]
    rows, width = line.shape[0] // LINE, line.shape[1]
    return pl.pallas_call(
        assemble_kernel,
        grid_spec=pltpu.PrefetchScalarGridSpec(
            num_scalar_prefetch=1,
            grid=(LINE,),
            in_specs=[pl.BlockSpec((rows, width), lambda i, place: (i, 0))] * len(parts),
            out_specs=pl.BlockSpec((len(parts) * rows, width), lambda i, place: (i, 0)),
        ),
        out_shape=jax.ShapeDtypeStruct((len(parts) * line.shape[0], width), line.dtype),
        cost_estimate=cost(0, 16 * line.size),
        compiler_params=pltpu.CompilerParams(vmem_limit_bytes=24 * 1024 * 1024),
        name="assemble",
    )(jnp.stack(place).astype(jnp.int32), *parts)


def add_rounded(a, b):
    return (a.astype(F32) + b.astype(F32)).astype(BF16)


def scatter_chip(near, far):
    if not blocks_known():
        return jnp.concatenate([near, far], 0)
    return add_rounded(near, hop(far, "core"))


def scatter_pair(chip):
    if not blocks_known():
        return chip
    half = chip.shape[0] // WIDE
    return add_rounded(chip[:half], hop(chip[half:], "x"))


def scatter_line(pair):
    if not blocks_known():
        return lax.psum_scatter(pair, "seq", scatter_dimension=0, tiled=True).astype(F32)
    parts = along_line(pair).reshape(LINE, -1, pair.shape[1])
    return jnp.sum(parts.astype(F32), axis=0)


def hop_sums(vec, plan):
    for axis, steps in plan:
        size = lax.axis_size(axis)
        if axis == "tp":
            steps = tuple(2**i for i in range(size.bit_length() - 1))
        if steps == (4, 8):
            steps = tuple(2**i for i in range(2, size.bit_length() - 1))
        for step in steps:
            vec = vec + lax.ppermute(vec, axis, [(i, i ^ step) for i in range(size)])
    return vec


def shards(
    layer_input,
    attn_gain,
    w_qkv,
    w_out,
    mlp_gain,
    w_up,
    w_down,
    w_unpatch,
    dens_in,
    dens_bias,
    dens_out,
    color_in,
    color_bias,
    color_out,
    edge_ids,
    blend_steps,
    live_count,
    color_grad,
    out_grad,
):
    tp_count = lax.axis_size("tp")
    tp_index = lax.axis_index("tp")
    length, model_width = layer_input.shape
    own_rows = length // tp_count
    own_tri = TRI // tp_count
    own_rest = own_rows - own_tri
    slab_planes = GRID // tp_count
    slab_edges = edge_ids.shape[1]

    def split_rows(x):
        blocks = x.reshape(tp_count, own_rows, x.shape[-1])
        return (
            blocks[:, own_rest:].reshape(TRI, x.shape[-1]),
            blocks[:, :own_rest].reshape(length - TRI, x.shape[-1]),
        )

    def block_rows(x):
        tri = x[:TRI].reshape(tp_count, own_tri, x.shape[-1])
        rest = x[TRI:].reshape(tp_count, own_rest, x.shape[-1])
        return jnp.concatenate([rest, tri], 1).reshape(length, x.shape[-1])

    def own_columns(x, width):
        if width == x.shape[1]:
            return x
        return lax.dynamic_slice_in_dim(x, tp_index * width, width, 1)

    def own_of(rows, count):
        return lax.dynamic_slice_in_dim(rows, tp_index * count, count, 0)

    packed = jnp.concatenate(
        [
            edge_ids.astype(F32),
            blend_steps.astype(F32),
            jnp.broadcast_to(live_count.astype(F32), edge_ids.shape),
            color_grad[:, 0],
        ],
        0,
    )
    slabs = tp_rows(packed).reshape(tp_count, packed.shape[0], slab_edges)
    spots, edges = edge_tables(
        slabs[:, 0].astype(jnp.int32), slabs[:, 1], slabs[:, 2, :1].astype(jnp.int32), slab_planes
    )
    cot = slabs[:, 3:].swapaxes(0, 1).reshape(-1, tp_count * slab_edges)
    cot = jnp.pad(cot, ((0, 8 - cot.shape[0]), (0, 0)))

    places = own_places(model_width // 64)
    in_order = jnp.arange(model_width // 64, dtype=jnp.int32)
    x_tri, x_rest = split_rows(layer_input)
    rows_in = jnp.concatenate([x_tri, x_rest], 0)
    og_tri, og_rest = split_rows(out_grad)
    gm_rest = og_rest.astype(BF16)
    og_own = own_of(og_rest, own_rest)

    local_width = w_out.shape[0]
    first = gather_plain(jnp.concatenate([w_qkv.reshape(w_qkv.shape[0], -1), w_out.T], 1))
    first = after(first, spots, edges, cot, gm_rest, rows_in)
    if blocks_known():
        line_u = gather_line(w_up)
        first = after(first, line_u)
    else:
        line_u = w_up
    down_t = gather_plain(after(w_down.T, first))
    qkv_full, out_t = first[:, : 3 * local_width], first[:, 3 * local_width :]

    normed_a = layer_norm(rows_in.astype(F32), attn_gain).astype(BF16)
    projected = dot(normed_a, qkv_full).astype(BF16)
    attended, lse = attend_fwd(projected, local_width)
    if blocks_known():
        wide_u = hop(line_u, "x")
        up_full = gather_rest(line_u, wide_u)
    else:
        wide_u = line_u
        up_full = gather_plain(w_up)
    rest_own = own_of(x_rest, own_rest).astype(F32)
    out_tri = dot(attended[:TRI], out_t, NT)
    mine, theirs = tp_parts(dot(after(attended, out_tri)[TRI:], out_t, NT))
    hidden_tri = x_tri.astype(F32) + tp_sum(out_tri, theirs)
    hidden_rest = rest_own + tp_sum_own(mine, theirs)

    normed_own = layer_norm(hidden_rest, mlp_gain).astype(BF16)
    unpatch_full = gather_plain(after(w_unpatch, hidden_tri, normed_own, wide_u))

    normed_tri = layer_norm(hidden_tri, mlp_gain).astype(BF16)
    tokens = (hidden_tri + tp_sum(mlp_tri(normed_tri, up_full, down_t))).astype(BF16)
    normed_rest = tp_rows(normed_own)

    act_rest, gup_rest = mlp_mid(normed_rest, gm_rest, up_full, down_t)
    gnb_mine, gnb_theirs = tp_parts(dot(gup_rest, up_full, NT))
    tokens = after(tokens, gnb_theirs)

    (
        colors_all,
        grad_units,
        grad_tokens,
        g_dens_in,
        g_dens_bias,
        g_dens_out,
        g_color_in,
        g_color_bias,
        g_color_out,
    ) = scene_pass(
        tokens,
        unpatch_full,
        spots,
        edges,
        cot,
        tp_index[None].astype(jnp.int32),
        (dens_in, dens_bias, dens_out, color_in, color_bias, color_out),
        slab_edges,
    )
    colors = lax.dynamic_slice_in_dim(
        colors_all[: color_out.shape[0]], tp_index * slab_edges, slab_edges, 1
    )
    gnb_rest = tp_sum_own(gnb_mine, gnb_theirs, grad_tokens)
    go_tri = og_tri + grad_tokens
    gm_tri = go_tri.astype(BF16)
    act_tri, gup_tri = mlp_mid(normed_tri, gm_tri, up_full, down_t)
    gnb_tri = tp_sum(dot(gup_tri, up_full, NT).astype(BF16))
    grad_down = weight_grad(in_order, 1, ((gm_rest, gm_tri), (act_rest, act_tri)))[0]
    sum_down = scatter_plain(grad_down).astype(F32)
    width = grad_units.shape[1] // tp_count if tp_count == 2 else grad_units.shape[1]
    sum_unpatch = scatter_plain(dot(tokens, own_columns(grad_units, width), TN).astype(BF16))
    grad_up = weight_grad(places, 2, ((normed_rest, normed_tri), (gup_rest, gup_tri)))
    _, back_rest = jax.vjp(layer_norm, hidden_rest, mlp_gain)
    gh_rest, gain_rest = back_rest(gnb_rest)
    _, back_tri = jax.vjp(lambda h: layer_norm(h, mlp_gain), hidden_tri)
    gh_tri = back_tri(gnb_tri)[0] + go_tri
    _, back_gain = jax.vjp(lambda g: layer_norm(own_of(hidden_tri, own_tri), g), mlp_gain)
    grad_mlp_gain = gain_rest + back_gain(own_of(gnb_tri, own_tri))[0]
    gh_rest = gh_rest + og_own
    branch = jnp.concatenate([gh_tri.astype(BF16), tp_rows(gh_rest.astype(BF16))], 0)

    chip_up = scatter_chip(*grad_up)
    grad_heads = dot(branch, out_t).astype(BF16)
    grad_heads = after(grad_heads, chip_up, grad_down)
    pair_up = scatter_pair(chip_up)
    grad_proj = attend_bwd(projected, grad_heads, attended, lse, local_width)
    grad_proj = after(grad_proj, pair_up)
    sum_up = scatter_line(pair_up)
    chip_last = scatter_chip(
        *weight_grad(places, 2, ((normed_a,), (grad_proj,)), ((branch,), (attended,)), room=60)
    )
    pair_last = scatter_pair(chip_last)
    gna = dot(after(grad_proj, chip_last), qkv_full, NT)
    gna_mine, gna_theirs = tp_parts(block_rows(gna))
    gna_sum = tp_sum_own(gna_mine, gna_theirs)
    sum_last = scatter_line(pair_last)
    _, back_gain_a = jax.vjp(lambda g: layer_norm(rows_in.astype(F32), g), attn_gain)
    grad_attn_gain = back_gain_a(gna)[0]
    tri_own = own_of(x_tri, own_tri).astype(F32)
    _, back_a = jax.vjp(
        lambda v: layer_norm(v, attn_gain), jnp.concatenate([rest_own, tri_own], 0)
    )
    grad_input = back_a(gna_sum)[0] + jnp.concatenate(
        [gh_rest, own_of(gh_tri, own_tri)], 0
    )
    if tp_count == 2:
        other = swap(sum_unpatch)
        low = tp_index == 0
        sum_unpatch = jnp.concatenate(
            [jnp.where(low, sum_unpatch, other), jnp.where(low, other, sum_unpatch)], 1
        )
    sum_unpatch = sum_unpatch.astype(F32)

    weight_sums = (
        sum_last[:, : 3 * local_width].reshape(w_qkv.shape),
        sum_last[:, 3 * local_width :].T,
        sum_up,
        sum_down.T,
        sum_unpatch,
    )
    smalls = (
        grad_attn_gain,
        grad_mlp_gain,
        g_dens_in,
        g_dens_bias,
        g_dens_out,
        g_color_in,
        g_color_bias,
        g_color_out[: color_out.shape[0]],
    )
    flat = jnp.concatenate([s.reshape(-1) for s in smalls])
    flat = after(hop_sums(after(flat, gna_theirs), (("seq", (4, 8)), ("seq", (1,)))), pair_last)
    flat = hop_sums(flat, (("tp", (1,)), ("seq", (2,))))
    small_sums = []
    at = 0
    for s in smalls:
        small_sums.append(flat[at : at + s.size].reshape(s.shape))
        at += s.size
    for i in (3, 4, 6):
        small_sums[i] = small_sums[i].reshape(-1)
    return (
        colors[:, None, :],
        grad_input,
        small_sums[0],
        weight_sums[0],
        weight_sums[1],
        small_sums[1],
        weight_sums[2],
        weight_sums[3],
        weight_sums[4],
        small_sums[2],
        small_sums[3],
        small_sums[4],
        small_sums[5],
        small_sums[6],
        small_sums[7],
    )


def solution(mesh):
    placed = (
        P("seq", None),
        P(),
        P("seq", None, "tp"),
        P("tp", "seq"),
        P(),
        P("seq", "tp"),
        P("tp", "seq"),
        P("seq", None),
        P(),
        P(),
        P(),
        P(),
        P(),
        P(),
        P("seq", "tp"),
        P("seq", "tp"),
        P("seq", "tp"),
        P(None, "seq", "tp"),
        P("seq", None),
    )
    return jax.shard_map(
        shards,
        mesh=mesh,
        in_specs=placed,
        out_specs=(
            P(None, "seq", "tp"),
            P(("seq", "tp"), None),
            P(),
            P("seq", None, "tp"),
            P("tp", "seq"),
            P(),
            P("seq", "tp"),
            P("tp", "seq"),
            P("seq", None),
            P(),
            P(),
            P(),
            P(),
            P(),
            P(),
        ),
        check_vma=False,
    )
```

```python
import functools
import math

import jax
import jax.numpy as jnp
from jax import lax
from jax.experimental import pallas as pl
from jax.experimental.pallas import tpu as pltpu
from jax.sharding import PartitionSpec as P

HEAD_DIM = 64
FEAT = 32
PATCH = 8
GRID = 64
TRI = 192
SIDE = GRID // PATCH
PLANE_TOKENS = SIDE * SIDE
SPOTS = PLANE_TOKENS * PATCH
CELLS = PATCH * FEAT

HIGHEST = lax.Precision.HIGHEST
BF16 = jnp.bfloat16
F32 = jnp.float32
NN = (((1,), (0,)), ((), ()))
NT = (((1,), (1,)), ((), ()))
TN = (((0,), (0,)), ((), ()))


def cost(flops, moved, exps=0):
    return pl.CostEstimate(flops=int(flops), bytes_accessed=int(moved), transcendentals=int(exps))


def dot(a, b, dims=NN, precision=None):
    return lax.dot_general(a, b, dims, precision=precision, preferred_element_type=F32)


def gelu_parts(x):
    density = jnp.exp(-0.5 * x * x)
    t = 1.0 / (1.0 + (0.3275911 * 2.0**-0.5) * jnp.abs(x))
    poly = ((((1.061405429 * t - 1.453152027) * t + 1.421413741) * t - 0.284496736) * t + 0.254829592) * t
    tail = 0.5 * poly * density
    cdf = jnp.where(x < 0.0, tail, 1.0 - tail)
    return x * cdf, cdf + x * (density * (1.0 / math.sqrt(2.0 * math.pi)))


def leave(*refs):
    pass


def after(x, *others):
    if not others:
        return x
    anywhere = pl.BlockSpec(memory_space=pl.ANY)
    return pl.pallas_call(
        leave,
        in_specs=[anywhere] * (1 + len(others)),
        out_specs=anywhere,
        out_shape=jax.ShapeDtypeStruct(x.shape, x.dtype),
        input_output_aliases={0: 0},
        name="after",
    )(x, *others)


def layer_norm(values, gain_vec):
    center = values - jnp.mean(values, axis=-1, keepdims=True)
    spread = jnp.mean(center * center, axis=-1, keepdims=True)
    return center * lax.rsqrt(spread + 1e-05) * gain_vec


def attend_fwd_kernel(q_ref, k_ref, v_ref, o_ref, lse_ref, *, scale, block):
    length, width = q_ref.shape
    heads = width // HEAD_DIM
    lane = lax.broadcasted_iota(jnp.int32, (1, width), 1) // HEAD_DIM
    lane_block = lax.broadcasted_iota(jnp.int32, (block, width), 1)
    keys = k_ref[...]
    values = v_ref[...]
    zero = jnp.zeros((), BF16)
    masked = [jnp.where(lane == h, keys, zero) for h in range(heads)]
    for b in range(length // block):
        rows = pl.ds(b * block, block)
        q = (q_ref[rows, :].astype(F32) * scale).astype(BF16)
        result = jnp.zeros((block, width), F32)
        stats = jnp.zeros((block, width), F32)
        for h in range(heads):
            s = dot(q, masked[h], NT)
            top = jnp.max(s, axis=1, keepdims=True)
            p = jnp.exp(s - top)
            total = jnp.sum(p, axis=1, keepdims=True)
            o = dot((p * (1.0 / total)).astype(BF16), values)
            result = jnp.where(lane == h, o, result)
            stats = jnp.where(lane_block == h, top + jnp.log(total), stats)
        o_ref[rows, :] = result.astype(BF16)
        lse_ref[0, :, pl.ds(b * block, block)] = stats.T[:8, :]


def attend_fwd(projected, local_width):
    length = projected.shape[0]
    width = 2 * HEAD_DIM
    pairs = local_width // width
    spec = lambda part: pl.BlockSpec((length, width), lambda i: (0, part * pairs + i))
    return pl.pallas_call(
        functools.partial(attend_fwd_kernel, scale=HEAD_DIM**-0.5, block=512),
        grid=(pairs,),
        in_specs=[spec(0), spec(1), spec(2)],
        out_specs=[
            pl.BlockSpec((length, width), lambda i: (0, i)),
            pl.BlockSpec((1, 8, length), lambda i: (i, 0, 0)),
        ],
        out_shape=[
            jax.ShapeDtypeStruct((length, local_width), BF16),
            jax.ShapeDtypeStruct((pairs, 8, length), F32),
        ],
        compiler_params=pltpu.CompilerParams(vmem_limit_bytes=48 * 1024 * 1024),
        cost_estimate=cost(
            12 * length * length * local_width, 8 * length * local_width, length * length * pairs * 2
        ),
        name="attend_fwd",
    )(projected, projected, projected)


def attend_bwd_kernel(
    q_ref, k_ref, v_ref, g_ref, o_ref, lse_ref, out_ref, dq_ref, dk_ref, dv_ref, *, scale, block
):
    length, width = q_ref.shape
    heads = width // HEAD_DIM
    step = pl.program_id(1)

    @pl.when(step == 0)
    def _():
        lane = lax.broadcasted_iota(jnp.int32, (1, width), 1) // HEAD_DIM
        keys = k_ref[...]
        values = v_ref[...]
        zero = jnp.zeros((), BF16)
        key_cols = keys.T
        prod = g_ref[...].astype(F32) * o_ref[...].astype(F32)
        pick = (
            lax.broadcasted_iota(jnp.int32, (8, width), 1) // HEAD_DIM
            == lax.broadcasted_iota(jnp.int32, (8, width), 0)
        ).astype(F32)
        inner = dot(pick, prod, NT, HIGHEST)
        for h in range(heads):
            k_h = jnp.where(lane == h, keys, zero)
            v_h = jnp.where(lane == h, values, zero)
            for b in range(length // block):
                rows = pl.ds(b * block, block)
                q = (q_ref[rows, :].astype(F32) * scale).astype(BF16)
                g = g_ref[rows, :]
                s = dot(k_h, q, NT)
                p = jnp.exp(s - lse_ref[0, h : h + 1, b * block : (b + 1) * block])
                dp = dot(v_h, g, NT)
                ds = (p * (dp - inner[h : h + 1, b * block : (b + 1) * block])).astype(BF16)
                dv = dot(p.astype(BF16), jnp.where(lane == h, g, zero))
                dk = dot(ds, jnp.where(lane == h, q, zero))
                if h == 0 and b == 0:
                    dv_ref[...] = dv
                    dk_ref[...] = dk
                else:
                    dv_ref[...] += dv
                    dk_ref[...] += dk
                dq_ref[h * HEAD_DIM : (h + 1) * HEAD_DIM, b * block : (b + 1) * block] = (
                    dot(key_cols[h * HEAD_DIM : (h + 1) * HEAD_DIM, :], ds) * scale
                )
        out_ref[...] = dq_ref[...].T.astype(BF16)

    @pl.when(step == 1)
    def _():
        out_ref[...] = dk_ref[...].astype(BF16)

    @pl.when(step == 2)
    def _():
        out_ref[...] = dv_ref[...].astype(BF16)


def attend_bwd(projected, grad_heads, attended, lse, local_width):
    length = projected.shape[0]
    width = 2 * HEAD_DIM
    pairs = local_width // width
    spec = lambda part: pl.BlockSpec((length, width), lambda i, j: (0, part * pairs + i))
    return pl.pallas_call(
        functools.partial(attend_bwd_kernel, scale=HEAD_DIM**-0.5, block=256),
        grid=(pairs, 3),
        in_specs=[
            spec(0),
            spec(1),
            spec(2),
            spec(0),
            spec(0),
            pl.BlockSpec((1, 8, length), lambda i, j: (i, 0, 0)),
        ],
        out_specs=pl.BlockSpec((length, width), lambda i, j: (0, j * pairs + i)),
        out_shape=jax.ShapeDtypeStruct((length, 3 * local_width), BF16),
        scratch_shapes=[
            pltpu.VMEM((width, length), F32),
            pltpu.VMEM((length, width), F32),
            pltpu.VMEM((length, width), F32),
        ],
        compiler_params=pltpu.CompilerParams(vmem_limit_bytes=48 * 1024 * 1024),
        cost_estimate=cost(
            24 * length * length * local_width, 16 * length * local_width, length * length * pairs * 2
        ),
        name="attend_bwd",
    )(projected, projected, projected, grad_heads, attended, lse)


def mlp_mid_kernel(nb_ref, gm_ref, up_ref, down_ref, act_ref, gup_ref, *back, block):
    up = up_ref[...]
    down = down_ref[...]
    for b in range(nb_ref.shape[0] // block):
        rows = pl.ds(b * block, block)
        value, slope = gelu_parts(dot(nb_ref[rows, :], up))
        act_ref[rows, :] = value.astype(BF16)
        gup_ref[rows, :] = (slope * dot(gm_ref[rows, :], down)).astype(BF16)
    for back_ref in back:
        part = dot(gup_ref[...], up, NT)

        @pl.when(pl.program_id(0) == 0)
        def _():
            back_ref[...] = part

        @pl.when(pl.program_id(0) > 0)
        def _():
            back_ref[...] += part


def mlp_mid(normed, grad, up_full, down_full, back=False):
    rows, depth = normed.shape
    width = up_full.shape[1]
    cols = min(width, 512)
    block = rows
    for cand in (416, 192):
        if rows % cand == 0:
            block = cand
            break
    whole = pl.BlockSpec((rows, depth), lambda i: (0, 0))
    weight = pl.BlockSpec((depth, cols), lambda i: (0, i))
    result = pl.BlockSpec((rows, cols), lambda i: (0, i))
    return pl.pallas_call(
        functools.partial(mlp_mid_kernel, block=block),
        grid=(width // cols,),
        in_specs=[whole, whole, weight, weight],
        out_specs=[result, result] + [whole] * back,
        out_shape=[jax.ShapeDtypeStruct((rows, width), BF16)] * 2
        + [jax.ShapeDtypeStruct((rows, depth), F32)] * back,
        compiler_params=pltpu.CompilerParams(vmem_limit_bytes=60 * 1024 * 1024),
        cost_estimate=cost(
            8 * rows * depth * width, 4 * (rows + width) * depth + 4 * rows * width, rows * width
        ),
        name="mlp_mid",
    )(normed, grad, up_full, down_full)


def mlp_tri_kernel(nb_ref, up_ref, down_ref, out_ref):
    value, _ = gelu_parts(dot(nb_ref[...], up_ref[...]))
    part = dot(value.astype(BF16), down_ref[...], NT)

    @pl.when(pl.program_id(0) == 0)
    def _():
        out_ref[...] = part

    @pl.when(pl.program_id(0) > 0)
    def _():
        out_ref[...] += part


def mlp_tri(normed, up_full, down_full):
    rows, depth = normed.shape
    width = up_full.shape[1]
    cols = min(width, 512)
    whole = pl.BlockSpec((rows, depth), lambda i: (0, 0))
    weight = pl.BlockSpec((depth, cols), lambda i: (0, i))
    return pl.pallas_call(
        mlp_tri_kernel,
        grid=(width // cols,),
        in_specs=[whole, weight, weight],
        out_specs=whole,
        out_shape=jax.ShapeDtypeStruct((rows, depth), F32),
        compiler_params=pltpu.CompilerParams(vmem_limit_bytes=60 * 1024 * 1024),
        cost_estimate=cost(4e9, 4 * width * depth, rows * width),
        name="mlp_tri",
    )(normed, up_full, down_full)


def weight_grad_kernel(place_ref, *refs, segments, pieces):
    step = pl.program_id(0)
    rest = refs[2 * sum(n for n, _, _ in segments) :]
    outs, turned = rest[:pieces], rest[pieces:]
    at = 0
    for parts, first, last in segments:
        lefts, rights = refs[at : at + parts], refs[at + parts : at + 2 * parts]
        at += 2 * parts

        @pl.when(step == first)
        def _():
            for left, spot in zip(lefts, turned):
                rows = left.shape[0]
                for j in range(left.shape[1] // 128):
                    both = left[:, j * 128 : (j + 1) * 128].T
                    for k in range(2):
                        to = pl.multiple_of(place_ref[2 * j + k] * 64, 64)
                        spot[pl.ds(to, 64), :rows] = both[k * 64 : (k + 1) * 64]

        @pl.when((step >= first) & (step <= last))
        def _():
            total = sum(
                dot(spot[:, : right.shape[0]], right[...]) for spot, right in zip(turned, rights)
            )
            for i, out in enumerate(outs):
                rows = out.shape[0]
                out[...] = total[i * rows : (i + 1) * rows].astype(BF16)


def weight_grad(place, pieces, *segments, room=40):
    specs, args, marks = [], [], []
    first = 0
    cols = min(512, *(rights[0].shape[1] for _, rights in segments))
    depth = segments[0][0][0].shape[1]
    for lefts, rights in segments:
        steps = rights[0].shape[1] // cols
        for left in lefts:
            specs.append(pl.BlockSpec(left.shape, lambda i, place: (0, 0)))
            args.append(left)
        for right in rights:
            specs.append(
                pl.BlockSpec(
                    (right.shape[0], cols),
                    lambda i, place, a=first, b=steps: (0, jnp.clip(i - a, 0, b - 1)),
                )
            )
            args.append(right)
        marks.append((len(lefts), first, first + steps - 1))
        first += steps
    parts = segments[0][0]
    result = jax.ShapeDtypeStruct((depth // pieces, first * cols), BF16)
    return pl.pallas_call(
        functools.partial(weight_grad_kernel, segments=tuple(marks), pieces=pieces),
        grid_spec=pltpu.PrefetchScalarGridSpec(
            num_scalar_prefetch=1,
            grid=(first,),
            in_specs=specs,
            out_specs=[pl.BlockSpec((depth // pieces, cols), lambda i, place: (0, i))] * pieces,
            scratch_shapes=[pltpu.VMEM((depth, left.shape[0]), BF16) for left in parts],
        ),
        out_shape=[result] * pieces,
        compiler_params=pltpu.CompilerParams(vmem_limit_bytes=room * 1024 * 1024),
        cost_estimate=cost(
            3 * depth * first * cols * sum(left.shape[0] for left in parts), 8 * depth * first * cols
        ),
        name="weight_grad",
    )(place, *args)


def split_halves(x):
    high = x.astype(BF16)
    return high, (x - high.astype(F32)).astype(BF16)


def dot_fine(a, b):
    a_high, a_low = split_halves(a)
    b_high, b_low = split_halves(b)
    return dot(
        jnp.concatenate([a_high, a_high, a_low], axis=1),
        jnp.concatenate([b_high, b_low, b_high], axis=0),
    )


def dot_fine_lanes(a, b):
    rows, cols = a.shape[0], b.shape[0]
    both = dot(
        jnp.concatenate(split_halves(a), axis=0), jnp.concatenate(split_halves(b), axis=0), NT
    )
    return both[:rows, :cols] + both[:rows, cols:] + both[rows:, :cols]


def scene_kernel(
    own_ref,
    tokens_ref,
    w_ref,
    spot_ref,
    edge_ref,
    cot_ref,
    net_ref,
    colors_ref,
    units_ref,
    gtok_ref,
    gdi_ref,
    gdb_ref,
    gdo_ref,
    gci_ref,
    gcb_ref,
    gco_ref,
    table_ref,
    hot_ref,
    grad_ref,
    *,
    per_slab,
):
    step = pl.program_id(0)
    block = spot_ref.shape[1]
    ends = 2 * block

    @pl.when(step == 0)
    def _():
        units = dot(tokens_ref[...], w_ref[...])
        for p in range(3):
            rows = jnp.concatenate(
                [
                    units[p * PLANE_TOKENS : (p + 1) * PLANE_TOKENS, r * CELLS : (r + 1) * CELLS]
                    for r in range(PATCH)
                ],
                axis=0,
            )
            high, low = split_halves(rows.T)
            table_ref[p, :CELLS, :] = high
            table_ref[p, CELLS:, :] = low
        grad_ref[...] = jnp.zeros_like(grad_ref)
        for ref in (gdi_ref, gdb_ref, gdo_ref, gci_ref, gcb_ref, gco_ref):
            ref[...] = jnp.zeros_like(ref)

    net = net_ref[...]
    dens_in, color_in = net[:, :FEAT], net[:, FEAT : 2 * FEAT]
    color_out_t = net[:, 2 * FEAT : 2 * FEAT + 8]
    at = 2 * FEAT + 8
    dens_bias, dens_out, color_bias = net[:, at : at + 1], net[:, at + 1 : at + 2], net[:, at + 2 : at + 3]
    dens_in_t, color_in_t, color_out = dens_in.T, color_in.T, color_out_t.T
    iota = lax.broadcasted_iota(jnp.int32, (SPOTS, ends), 0)
    field = jnp.zeros((FEAT, ends), F32)
    columns = []
    for p in range(3):
        spot = jnp.concatenate([spot_ref[p : p + 1, :], spot_ref[3 + p : 4 + p, :]], axis=1)
        column = jnp.concatenate([spot_ref[6 + p : 7 + p, :], spot_ref[9 + p : 10 + p, :]], axis=1)
        columns.append(column)
        hot = jnp.where(iota == spot, 1.0, 0.0).astype(BF16)
        hot_ref[p] = hot
        found = dot(table_ref[p], hot)
        found = found[:CELLS] + found[CELLS:]
        for c in range(PATCH):
            field = field + jnp.where(column == c, found[c * FEAT : (c + 1) * FEAT], 0.0)

    w_a = edge_ref[0:1, :]
    w_b = edge_ref[1:2, :]
    inside = edge_ref[2:3, :]
    live = edge_ref[3:4, :]
    pre_d = dot_fine(dens_in, field) + dens_bias
    act_d, slope_d = gelu_parts(pre_d)
    dens = jnp.sum(act_d * dens_out, axis=0, keepdims=True)
    v_dens = w_a * dens[:, :block] + w_b * inside * dens[:, block:]
    v_feat = w_a * field[:, :block] + w_b * field[:, block:]
    pre_c = dot_fine(color_in, v_feat) + color_bias
    act_c, slope_c = gelu_parts(pre_c)
    shade = jax.nn.sigmoid(dot_fine(color_out, act_c))
    opacity = jax.nn.sigmoid(v_dens)
    colors_ref[...] = live * opacity * shade
    g_color = cot_ref[...] * live
    g_shade = g_color * opacity
    g_logit = g_shade * shade * (1.0 - shade)
    g_dens = jnp.sum(g_color * shade, axis=0, keepdims=True) * opacity * (1.0 - opacity)
    g_pre_c = dot_fine(color_out_t, g_logit) * slope_c
    g_feat = dot_fine(color_in_t, g_pre_c)
    g_dens2 = jnp.concatenate([w_a * g_dens, w_b * inside * g_dens], axis=1)
    g_pre_d = dens_out * g_dens2 * slope_d
    g_field = dot_fine(dens_in_t, g_pre_d) + jnp.concatenate(
        [w_a * g_feat, w_b * g_feat], axis=1
    )

    @pl.when(step // per_slab == own_ref[0])
    def _():
        gco_ref[...] += dot_fine_lanes(g_logit, act_c)
        gci_ref[...] += dot_fine_lanes(g_pre_c, v_feat)
        gcb_ref[...] += jnp.sum(g_pre_c, axis=1, keepdims=True)
        gdi_ref[...] += dot_fine_lanes(g_pre_d, field)
        gdb_ref[...] += jnp.sum(g_pre_d, axis=1, keepdims=True)
        gdo_ref[...] += jnp.sum(act_d * g_dens2, axis=1, keepdims=True)

    for p in range(3):
        spread = jnp.concatenate(
            [jnp.where(columns[p] == c, g_field, 0.0) for c in range(PATCH)], axis=0
        )
        grad_ref[p] += dot(hot_ref[p], spread.astype(BF16), NT)

    @pl.when(step == pl.num_programs(0) - 1)
    def _():
        for p in range(3):
            for r in range(PATCH):
                units_ref[
                    p * PLANE_TOKENS : (p + 1) * PLANE_TOKENS, r * CELLS : (r + 1) * CELLS
                ] = grad_ref[p, r * PLANE_TOKENS : (r + 1) * PLANE_TOKENS, :].astype(BF16)
        gtok_ref[...] = dot(units_ref[...], w_ref[...], NT)


def scene_pass(tokens, w_unpatch, spots, edges, cot, own, small, slab_edges):
    dens_in, dens_bias, dens_out, color_in, color_bias, color_out = small
    net = jnp.concatenate(
        [
            dens_in,
            color_in,
            jnp.pad(color_out.T, ((0, 0), (0, 8 - color_out.shape[0]))),
            dens_bias[:, None],
            dens_out[:, None],
            color_bias[:, None],
        ],
        axis=1,
    )
    net = jnp.pad(net, ((0, 0), (0, 128 - net.shape[1])))
    total = spots.shape[1]
    block = min(512, slab_edges)
    const = lambda shape: pl.BlockSpec(shape, lambda i, own: (0,) * len(shape))
    lanes = lambda rows: pl.BlockSpec((rows, block), lambda i, own: (0, i))
    dens, colr = dens_in.shape[0], color_in.shape[0]
    outs = [
        ((8, total), F32, lanes(8)),
        ((TRI, w_unpatch.shape[1]), BF16, None),
        ((TRI, w_unpatch.shape[0]), F32, None),
        ((dens, FEAT), F32, None),
        ((dens, 1), F32, None),
        ((dens, 1), F32, None),
        ((colr, FEAT), F32, None),
        ((colr, 1), F32, None),
        ((8, colr), F32, None),
    ]
    return pl.pallas_call(
        functools.partial(scene_kernel, per_slab=slab_edges // block),
        grid_spec=pltpu.PrefetchScalarGridSpec(
            num_scalar_prefetch=1,
            grid=(total // block,),
            in_specs=[
                const(tokens.shape),
                const(w_unpatch.shape),
                lanes(16),
                lanes(8),
                lanes(8),
                const((dens, 128)),
            ],
            out_specs=[s if s is not None else const(shape) for shape, _, s in outs],
            scratch_shapes=[
                pltpu.VMEM((3, 2 * CELLS, SPOTS), BF16),
                pltpu.VMEM((3, SPOTS, 2 * block), BF16),
                pltpu.VMEM((3, SPOTS, CELLS), F32),
            ],
        ),
        out_shape=[jax.ShapeDtypeStruct(shape, kind) for shape, kind, _ in outs],
        compiler_params=pltpu.CompilerParams(vmem_limit_bytes=60 * 1024 * 1024),
        cost_estimate=cost(25e9, 8 * w_unpatch.size, 1e6),
        name="scene",
    )(
        own,
        tokens,
        w_unpatch,
        spots,
        edges,
        cot,
        net,
    )


def edge_tables(edge_rows, blend_rows, live_counts, slab_planes):
    slabs, count = edge_rows.shape
    plane_cells = GRID * GRID
    slab_cells = slab_planes * plane_cells
    direction = edge_rows // slab_cells
    cell = edge_rows % slab_cells
    first = (jnp.arange(slabs, dtype=jnp.int32) * slab_planes)[:, None]
    i_a = cell // plane_cells + first
    j_a = (cell % plane_cells) // GRID
    l_a = cell % GRID
    i_b = i_a + (direction == 0)
    j_b = j_a + (direction == 1)
    l_b = l_a + (direction == 2)
    valid = (j_b < GRID) & (l_b < GRID)
    inside = valid & (i_b < GRID)

    def place(row, col, keep):
        spot = (row % PATCH) * PLANE_TOKENS + (row // PATCH) * SIDE + col // PATCH
        return jnp.where(keep, spot, -1), col % PATCH

    on = jnp.ones_like(valid)
    pairs = [
        place(i_a, j_a, on),
        place(i_a, l_a, on),
        place(j_a, l_a, on),
        place(i_b, j_b, inside),
        place(i_b, l_b, inside),
        place(j_b, l_b, inside),
    ]
    blank_i = jnp.zeros_like(edge_rows)
    spots = jnp.stack([a for a, _ in pairs] + [b for _, b in pairs] + [blank_i] * 4)
    w_b = blend_rows.astype(F32) / 16.0
    w_a = 1.0 - w_b
    live = jnp.arange(count, dtype=jnp.int32)[None, :] < live_counts
    blank = jnp.zeros_like(w_b)
    edges = jnp.stack(
        [w_a, w_b * valid.astype(F32), inside.astype(F32), live.astype(F32)] + [blank] * 4
    )
    return spots.reshape(16, slabs * count), edges.reshape(8, slabs * count)


def swap(x, axis="tp"):
    return lax.ppermute(x, axis, [(0, 1), (1, 0)])


def tp_sum(partial, *gates):
    if lax.axis_size("tp") == 2:
        return partial.astype(F32) + after(swap(partial), *gates).astype(F32)
    return lax.psum(partial.astype(F32), "tp")


def tp_parts(partial):
    count = lax.axis_size("tp")
    if count != 2:
        return partial, partial
    rows = partial.shape[0] // count
    me = lax.axis_index("tp")
    theirs = lax.dynamic_slice_in_dim(partial, (1 - me) * rows, rows, 0).astype(BF16)
    return lax.dynamic_slice_in_dim(partial, me * rows, rows, 0), theirs


def tp_sum_own(mine, theirs, *gates):
    if lax.axis_size("tp") == 2:
        return mine + after(swap(theirs), *gates).astype(F32)
    return lax.psum_scatter(mine, "tp", scatter_dimension=0, tiled=True)


def tp_rows(own):
    if lax.axis_size("tp") == 2:
        other = swap(own)
        first = lax.axis_index("tp") == 0
        return jnp.concatenate(
            [jnp.where(first, own, other), jnp.where(first, other, own)], axis=0
        )
    return lax.all_gather(own, "tp", axis=0, tiled=True)


LINE, WIDE, CORES = 4, 2, 2


def blocks_known():
    return lax.axis_size("seq") == LINE * WIDE * CORES


def own_places(blocks):
    block = jnp.arange(blocks, dtype=jnp.int32)
    if not blocks_known():
        return block
    me = lax.axis_index("seq")
    w, c = (me // CORES) % WIDE, me % CORES
    z, x, core = block // (WIDE * CORES), (block // CORES) % WIDE, block % CORES
    return ((core ^ c) * WIDE + (x ^ w)) * LINE + z


def hop(x, kind):
    pairs = []
    for i in range(LINE * WIDE * CORES):
        z, w, c = i // (WIDE * CORES), (i // CORES) % WIDE, i % CORES
        if kind == "core":
            c = 1 - c
        else:
            w = 1 - w
        pairs.append((i, (z * WIDE + w) * CORES + c))
    return lax.ppermute(x, "seq", pairs)


def along_line(x):
    step = WIDE * CORES
    groups = [[z * step + i for z in range(LINE)] for i in range(step)]
    return lax.all_to_all(x, "seq", 0, 0, axis_index_groups=groups, tiled=True)


def gather_plain(shard):
    return lax.all_gather(shard, "seq", axis=0, tiled=True)


def scatter_plain(grad):
    return lax.psum_scatter(grad, "seq", scatter_dimension=0, tiled=True)


def gather_line(shard):
    return along_line(jnp.concatenate([shard] * LINE, 0))


def assemble_kernel(place_ref, *refs):
    *parts, out_ref = refs
    for i, part in enumerate(parts):
        rows = part.shape[0]
        out_ref[pl.ds(pl.multiple_of(place_ref[i] * rows, rows), rows), :] = part[...]


def gather_rest(line, wide):
    me = lax.axis_index("seq")
    w, c = (me // CORES) % WIDE, me % CORES
    parts = [line, wide, hop(line, "core"), hop(wide, "core")]
    place = [(w ^ xr) * CORES + (c ^ cr) for cr in range(CORES) for xr in range(WIDE)]
    rows, width = line.shape[0] // LINE, line.shape[1]
    return pl.pallas_call(
        assemble_kernel,
        grid_spec=pltpu.PrefetchScalarGridSpec(
            num_scalar_prefetch=1,
            grid=(LINE,),
            in_specs=[pl.BlockSpec((rows, width), lambda i, place: (i, 0))] * len(parts),
            out_specs=pl.BlockSpec((len(parts) * rows, width), lambda i, place: (i, 0)),
        ),
        out_shape=jax.ShapeDtypeStruct((len(parts) * line.shape[0], width), line.dtype),
        cost_estimate=cost(0, 16 * line.size),
        compiler_params=pltpu.CompilerParams(vmem_limit_bytes=24 * 1024 * 1024),
        name="assemble",
    )(jnp.stack(place).astype(jnp.int32), *parts)


def add_rounded(a, b):
    return (a.astype(F32) + b.astype(F32)).astype(BF16)


def scatter_chip(near, far):
    if not blocks_known():
        return jnp.concatenate([near, far], 0)
    return add_rounded(near, hop(far, "core"))


def scatter_pair(chip):
    if not blocks_known():
        return chip
    half = chip.shape[0] // WIDE
    return add_rounded(chip[:half], hop(chip[half:], "x"))


def scatter_line(pair):
    if not blocks_known():
        return lax.psum_scatter(pair, "seq", scatter_dimension=0, tiled=True).astype(F32)
    parts = along_line(pair).reshape(LINE, -1, pair.shape[1])
    return jnp.sum(parts.astype(F32), axis=0)


def hop_sums(vec, plan):
    for axis, steps in plan:
        size = lax.axis_size(axis)
        if axis == "tp":
            steps = tuple(2**i for i in range(size.bit_length() - 1))
        if steps == (4, 8):
            steps = tuple(2**i for i in range(2, size.bit_length() - 1))
        for step in steps:
            vec = vec + lax.ppermute(vec, axis, [(i, i ^ step) for i in range(size)])
    return vec


def shards(
    layer_input,
    attn_gain,
    w_qkv,
    w_out,
    mlp_gain,
    w_up,
    w_down,
    w_unpatch,
    dens_in,
    dens_bias,
    dens_out,
    color_in,
    color_bias,
    color_out,
    edge_ids,
    blend_steps,
    live_count,
    color_grad,
    out_grad,
):
    tp_count = lax.axis_size("tp")
    tp_index = lax.axis_index("tp")
    length, model_width = layer_input.shape
    own_rows = length // tp_count
    own_tri = TRI // tp_count
    own_rest = own_rows - own_tri
    slab_planes = GRID // tp_count
    slab_edges = edge_ids.shape[1]

    def split_rows(x):
        blocks = x.reshape(tp_count, own_rows, x.shape[-1])
        return (
            blocks[:, own_rest:].reshape(TRI, x.shape[-1]),
            blocks[:, :own_rest].reshape(length - TRI, x.shape[-1]),
        )

    def block_rows(x):
        tri = x[:TRI].reshape(tp_count, own_tri, x.shape[-1])
        rest = x[TRI:].reshape(tp_count, own_rest, x.shape[-1])
        return jnp.concatenate([rest, tri], 1).reshape(length, x.shape[-1])

    def own_columns(x, width):
        if width == x.shape[1]:
            return x
        return lax.dynamic_slice_in_dim(x, tp_index * width, width, 1)

    def own_of(rows, count):
        return lax.dynamic_slice_in_dim(rows, tp_index * count, count, 0)

    packed = jnp.concatenate(
        [
            edge_ids.astype(F32),
            blend_steps.astype(F32),
            jnp.broadcast_to(live_count.astype(F32), edge_ids.shape),
            color_grad[:, 0],
        ],
        0,
    )
    slabs = tp_rows(packed).reshape(tp_count, packed.shape[0], slab_edges)
    spots, edges = edge_tables(
        slabs[:, 0].astype(jnp.int32), slabs[:, 1], slabs[:, 2, :1].astype(jnp.int32), slab_planes
    )
    cot = slabs[:, 3:].swapaxes(0, 1).reshape(-1, tp_count * slab_edges)
    cot = jnp.pad(cot, ((0, 8 - cot.shape[0]), (0, 0)))

    places = own_places(model_width // 64)
    in_order = jnp.arange(model_width // 64, dtype=jnp.int32)
    x_tri, x_rest = split_rows(layer_input)
    rows_in = jnp.concatenate([x_tri, x_rest], 0)
    og_tri, og_rest = split_rows(out_grad)
    gm_rest = og_rest.astype(BF16)
    og_own = own_of(og_rest, own_rest)

    local_width = w_out.shape[0]
    first = gather_plain(jnp.concatenate([w_qkv.reshape(w_qkv.shape[0], -1), w_out.T], 1))
    first = after(first, spots, edges, cot, gm_rest, rows_in)
    if blocks_known():
        line_u = gather_line(w_up)
        first = after(first, line_u)
    else:
        line_u = w_up
    down_t = gather_plain(after(w_down.T, first))
    qkv_full, out_t = first[:, : 3 * local_width], first[:, 3 * local_width :]

    normed_a = layer_norm(rows_in.astype(F32), attn_gain).astype(BF16)
    projected = dot(normed_a, qkv_full).astype(BF16)
    attended, lse = attend_fwd(projected, local_width)
    if blocks_known():
        wide_u = hop(line_u, "x")
        up_full = gather_rest(line_u, wide_u)
    else:
        wide_u = line_u
        up_full = gather_plain(w_up)
    rest_own = own_of(x_rest, own_rest).astype(F32)
    out_tri = dot(attended[:TRI], out_t, NT)
    mine, theirs = tp_parts(dot(after(attended, out_tri)[TRI:], out_t, NT))
    hidden_tri = x_tri.astype(F32) + tp_sum(out_tri, theirs)
    hidden_rest = rest_own + tp_sum_own(mine, theirs)

    normed_own = layer_norm(hidden_rest, mlp_gain).astype(BF16)
    unpatch_full = gather_plain(after(w_unpatch, hidden_tri, normed_own, wide_u))

    normed_tri = layer_norm(hidden_tri, mlp_gain).astype(BF16)
    tokens = (hidden_tri + tp_sum(mlp_tri(normed_tri, up_full, down_t))).astype(BF16)
    normed_rest = tp_rows(normed_own)

    act_rest, gup_rest = mlp_mid(normed_rest, gm_rest, up_full, down_t)
    gnb_mine, gnb_theirs = tp_parts(dot(gup_rest, up_full, NT))
    tokens = after(tokens, gnb_theirs)

    (
        colors_all,
        grad_units,
        grad_tokens,
        g_dens_in,
        g_dens_bias,
        g_dens_out,
        g_color_in,
        g_color_bias,
        g_color_out,
    ) = scene_pass(
        tokens,
        unpatch_full,
        spots,
        edges,
        cot,
        tp_index[None].astype(jnp.int32),
        (dens_in, dens_bias, dens_out, color_in, color_bias, color_out),
        slab_edges,
    )
    colors = lax.dynamic_slice_in_dim(
        colors_all[: color_out.shape[0]], tp_index * slab_edges, slab_edges, 1
    )
    gnb_rest = tp_sum_own(gnb_mine, gnb_theirs, grad_tokens)
    go_tri = og_tri + grad_tokens
    gm_tri = go_tri.astype(BF16)
    act_tri, gup_tri, back_part = mlp_mid(normed_tri, gm_tri, up_full, down_t, back=True)
    gnb_tri = tp_sum(back_part.astype(BF16))
    grad_down = weight_grad(in_order, 1, ((gm_rest, gm_tri), (act_rest, act_tri)))[0]
    sum_down = scatter_plain(grad_down).astype(F32)
    width = grad_units.shape[1] // tp_count if tp_count == 2 else grad_units.shape[1]
    sum_unpatch = scatter_plain(dot(tokens, own_columns(grad_units, width), TN))
    grad_up = weight_grad(places, 2, ((normed_rest, normed_tri), (gup_rest, gup_tri)))
    _, back_rest = jax.vjp(layer_norm, hidden_rest, mlp_gain)
    gh_rest, gain_rest = back_rest(gnb_rest)
    _, back_tri = jax.vjp(lambda h: layer_norm(h, mlp_gain), hidden_tri)
    gh_tri = back_tri(gnb_tri)[0] + go_tri
    _, back_gain = jax.vjp(lambda g: layer_norm(own_of(hidden_tri, own_tri), g), mlp_gain)
    grad_mlp_gain = gain_rest + back_gain(own_of(gnb_tri, own_tri))[0]
    gh_rest = gh_rest + og_own
    branch = jnp.concatenate([gh_tri.astype(BF16), tp_rows(gh_rest.astype(BF16))], 0)

    chip_up = scatter_chip(*grad_up)
    grad_heads = dot(branch, out_t).astype(BF16)
    grad_heads = after(grad_heads, chip_up, grad_down)
    pair_up = scatter_pair(chip_up)
    grad_proj = attend_bwd(projected, grad_heads, attended, lse, local_width)
    grad_proj = after(grad_proj, pair_up)
    sum_up = scatter_line(pair_up)
    chip_last = scatter_chip(
        *weight_grad(places, 2, ((normed_a,), (grad_proj,)), ((branch,), (attended,)), room=60)
    )
    pair_last = scatter_pair(chip_last)
    gna = dot(after(grad_proj, chip_last), qkv_full, NT)
    gna_mine, gna_theirs = tp_parts(block_rows(gna))
    gna_sum = tp_sum_own(gna_mine, gna_theirs)
    sum_last = scatter_line(pair_last)
    _, back_gain_a = jax.vjp(lambda g: layer_norm(rows_in.astype(F32), g), attn_gain)
    grad_attn_gain = back_gain_a(gna)[0]
    tri_own = own_of(x_tri, own_tri).astype(F32)
    _, back_a = jax.vjp(
        lambda v: layer_norm(v, attn_gain), jnp.concatenate([rest_own, tri_own], 0)
    )
    grad_input = back_a(gna_sum)[0] + jnp.concatenate(
        [gh_rest, own_of(gh_tri, own_tri)], 0
    )
    if tp_count == 2:
        other = swap(sum_unpatch)
        low = tp_index == 0
        sum_unpatch = jnp.concatenate(
            [jnp.where(low, sum_unpatch, other), jnp.where(low, other, sum_unpatch)], 1
        )
    sum_unpatch = sum_unpatch.astype(F32)

    weight_sums = (
        sum_last[:, : 3 * local_width].reshape(w_qkv.shape),
        sum_last[:, 3 * local_width :].T,
        sum_up,
        sum_down.T,
        sum_unpatch,
    )
    smalls = (
        grad_attn_gain,
        grad_mlp_gain,
        g_dens_in,
        g_dens_bias,
        g_dens_out,
        g_color_in,
        g_color_bias,
        g_color_out[: color_out.shape[0]],
    )
    flat = jnp.concatenate([s.reshape(-1) for s in smalls])
    flat = after(hop_sums(after(flat, gna_theirs), (("seq", (4, 8)), ("seq", (1,)))), pair_last)
    flat = hop_sums(flat, (("tp", (1,)), ("seq", (2,))))
    small_sums = []
    at = 0
    for s in smalls:
        small_sums.append(flat[at : at + s.size].reshape(s.shape))
        at += s.size
    for i in (3, 4, 6):
        small_sums[i] = small_sums[i].reshape(-1)
    return (
        colors[:, None, :],
        grad_input,
        small_sums[0],
        weight_sums[0],
        weight_sums[1],
        small_sums[1],
        weight_sums[2],
        weight_sums[3],
        weight_sums[4],
        small_sums[2],
        small_sums[3],
        small_sums[4],
        small_sums[5],
        small_sums[6],
        small_sums[7],
    )


def solution(mesh):
    placed = (
        P("seq", None),
        P(),
        P("seq", None, "tp"),
        P("tp", "seq"),
        P(),
        P("seq", "tp"),
        P("tp", "seq"),
        P("seq", None),
        P(),
        P(),
        P(),
        P(),
        P(),
        P(),
        P("seq", "tp"),
        P("seq", "tp"),
        P("seq", "tp"),
        P(None, "seq", "tp"),
        P("seq", None),
    )
    return jax.shard_map(
        shards,
        mesh=mesh,
        in_specs=placed,
        out_specs=(
            P(None, "seq", "tp"),
            P(("seq", "tp"), None),
            P(),
            P("seq", None, "tp"),
            P("tp", "seq"),
            P(),
            P("seq", "tp"),
            P("tp", "seq"),
            P("seq", None),
            P(),
            P(),
            P(),
            P(),
            P(),
            P(),
        ),
        check_vma=False,
    )
```
